256 devices in a mesh: dp: 8 (over x, z_hi), tensor: 32 (over y, z_lo, core).
Axes of the slice: x: 4, y: 4, z: 8 (z_hi: 2, z_lo: 4; z = z_hi * 4 + z_lo), core: 2. Of those that a mesh axis runs over, the one named last changes fastest.
Arguments:
- block_input: bfloat16 [3072, 6144], P('dp', 'tensor'), may hold values from -6 to 6
- output_gradient: bfloat16 [3072, 6144], P('dp', 'tensor'), may hold values from -6 to 6
- attn_grad: bfloat16 [3072, 6144], P('dp', 'tensor'), may hold values from -6 to 6
- layernorm_gain: float32 [6144], replicated, may hold values from 0.5 to 1.5
- w_in: bfloat16 [6144, 12288], P(None, 'tensor'), may hold values from -0.078125 to 0.078125
- w_out: bfloat16 [12288, 6144], P('tensor'), may hold values from -0.0546875 to 0.0546875
Outputs:
- input_gradient: bfloat16 [3072, 6144], P('dp', 'tensor')
- gain_gradient: float32 [6144], P('tensor')
- w_in_grad: float32 [6144, 12288], P('dp', 'tensor')
- w_out_grad: float32 [12288, 6144], P('tensor', 'dp')
The draws below stay inside these ranges and needn't reach their ends.
All inputs are finite; a program needn't handle non-finite values.
Results may differ from the reference program's by a relative error of at most 0.018.
Values may be sent and summed in bfloat16 or wider, within the bound.
A program may use at most 128 MiB of HBM per device.

```python
import math
import jax
import jax.numpy as jnp
from jax import lax

D = 6144
FF = 12288
TOKENS = 3072
N_TENSOR = 32


def strengthened(values, stream_key, source, target, parts, factor):
    def block_of(dim):
        return (jnp.arange(values.shape[dim]) // (values.shape[dim] // parts)).reshape((-1,) + (1,) * (values.ndim - 1 - dim))

    first = jax.random.permutation(stream_key, parts)[block_of(target)]
    second = (block_of(target) + parts // 2) % parts
    return jnp.where((block_of(source) == first) | (block_of(source) == second), factor * values, values)


def shard_levels(own_key, extent, cuts, least, high):
    level, own = 1.0, jax.random.fold_in(own_key, 6)
    for axis_at, parts in cuts:
        steps = jnp.exp(jax.random.uniform(jax.random.fold_in(own, axis_at), (parts,), jnp.float32, least / len(cuts), high / len(cuts)))
        level = level * jnp.repeat(steps, extent[axis_at] // parts).reshape([-1 if axis == axis_at else 1 for axis in range(len(extent))])
    return level


def centred(own_key, dims, scale, reach, cuts=(), dtype=jnp.bfloat16):
    values = scale * jax.random.normal(own_key, dims, jnp.float32)
    if cuts:
        values = values * shard_levels(own_key, dims, cuts, -0.22, 0.18)
    return jnp.clip(values, -reach, reach).astype(dtype)


def gaussian_with(own_key, shape, scale, limit, cuts, heavy, dtype=jnp.bfloat16):
    drawn = scale * jax.random.normal(own_key, shape, jnp.float32)
    if cuts:
        drawn = drawn * shard_levels(own_key, shape, cuts, -0.22, 0.18)
    return jnp.clip(strengthened(drawn, jax.random.fold_in(own_key, 3), *heavy), -limit, limit).astype(dtype)


def setup_inputs(seed: int = 0) -> dict:
    arg_keys = jax.random.split(jax.random.key(seed), 7)
    block_input = centred(arg_keys[0], (TOKENS, D), 1.0, 6.0, ((0, 8), (1, 32)))
    output_gradient = gaussian_with(arg_keys[1], (TOKENS, D), 1.0, 6.0, ((0, 8), (1, 32)), (0, 1, 32, 2.75))
    attn_grad = centred(arg_keys[2], (TOKENS, D), 1.0, 6.0, ((0, 8), (1, 32)))
    layernorm_gain = jnp.clip(1.0 + 0.1 * jax.random.normal(arg_keys[3], (D,), jnp.float32), 0.5, 1.5)
    w_in = centred(arg_keys[4], (D, FF), D ** -0.5, 0.078125, ((1, 32),))
    w_out = centred(arg_keys[5], (FF, D), FF ** -0.5, 0.0546875, ((0, 32),))
    return {"block_input": block_input, "output_gradient": output_gradient, "attn_grad": attn_grad, "layernorm_gain": layernorm_gain, "w_in": w_in, "w_out": w_out}


gelu_coef = math.sqrt(2.0 / math.pi)

def gelu_value(value):
    inner = gelu_coef * (value + 0.044715 * value * value * value)
    return 0.5 * value * (1.0 + jnp.tanh(inner))

def gelu_slope(value):
    inner = gelu_coef * (value + 0.044715 * value * value * value)
    tanh_val = jnp.tanh(inner)
    return 0.5 * (1.0 + tanh_val) + 0.5 * value * (1.0 - tanh_val * tanh_val) * gelu_coef * (1.0 + 3.0 * 0.044715 * value * value)

def reference(block_input, output_gradient, attn_grad, layernorm_gain, w_in, w_out):
    values = block_input.astype(jnp.float32)
    row_mean = lax.optimization_barrier(jnp.mean(values, axis=1, keepdims=True))
    centered_input = values - row_mean
    variance = lax.optimization_barrier(jnp.mean(centered_input * centered_input, axis=1, keepdims=True))
    inverse_deviation = lax.rsqrt(variance + 1e-06)
    standardized_input = centered_input * inverse_deviation
    normalized_input = (standardized_input * layernorm_gain).astype(jnp.bfloat16)
    pre_act = jnp.dot(normalized_input, w_in, preferred_element_type=jnp.float32)
    hidden_act = gelu_value(pre_act).astype(jnp.bfloat16)
    act_grad = jnp.dot(output_gradient, w_out.T, preferred_element_type=jnp.float32)
    hidden_grad = (act_grad * gelu_slope(pre_act)).astype(jnp.bfloat16)
    w_out_grad = jnp.dot(hidden_act.T, output_gradient, preferred_element_type=jnp.float32)
    w_in_grad = jnp.dot(normalized_input.T, hidden_grad, preferred_element_type=jnp.float32)
    block_width = FF // N_TENSOR
    grad_blocks = jnp.transpose(hidden_grad.reshape(TOKENS, N_TENSOR, block_width), (1, 0, 2))
    weight_blocks = jnp.transpose(w_in.reshape(D, N_TENSOR, block_width), (1, 0, 2))

    def accumulate(total, pieces):
        term = jnp.dot(pieces[0], pieces[1].T, preferred_element_type=jnp.float32)
        return (total + term.astype(jnp.bfloat16).astype(jnp.float32), None)
    summed, _ = lax.scan(accumulate, jnp.zeros((TOKENS, D), jnp.float32), (grad_blocks, weight_blocks))
    normalized_gradient = summed + attn_grad.astype(jnp.float32)
    scaled_gradient = normalized_gradient * layernorm_gain
    first_moment = lax.optimization_barrier(jnp.mean(scaled_gradient, axis=1, keepdims=True))
    second_moment = lax.optimization_barrier(jnp.mean(scaled_gradient * standardized_input, axis=1, keepdims=True))
    input_gradient = (output_gradient.astype(jnp.float32) + (scaled_gradient - first_moment - standardized_input * second_moment) * inverse_deviation).astype(jnp.bfloat16)
    gain_gradient = lax.optimization_barrier(jnp.sum(normalized_gradient * standardized_input, axis=0))
    return (input_gradient, gain_gradient, w_in_grad, w_out_grad)
```

```python
import functools
import math

import jax
import jax.numpy as jnp
from jax import lax
from jax.experimental import pallas as pl
from jax.experimental.pallas import tpu as pltpu
from jax.sharding import PartitionSpec as P

MESH = pl.DeviceIdType.MESH
F32, BF16 = jnp.float32, jnp.bfloat16
COEF = math.sqrt(2.0 / math.pi)
TOK = 384
HID = 384
ROWS = 192
CHIP = 384
D = 6144

NT = (((1,), (1,)), ((), ()))


def dot(a, b):
    return jnp.dot(a, b, preferred_element_type=F32)


def dot_nt(a, b):
    return lax.dot_general(a, b, NT, preferred_element_type=F32)


def wide(column):
    return jnp.concatenate([column] * (TOK // 128), axis=1)


def kernel(
    x_in, g_in, attn, gain, w_in, w_out,
    dx_out, gg_out, dwin_out, dwout_out,
    XG, XS, XN, WI, WT, WO, HB, GB, PRE, ACT, SM, SV, ST, R1, R2, R3, R4, TS, MO, GP,
    zs, zr, as_, ar, z2s, z2r, a2s, a2r, ps, pr, hs, hr, z4s, z4r, xs, xr, xbs, xbr,
    r1s, r1r, r2s, r2r, r3s, r3r, r4s, r4r, sts, str_, mos, mor, gps, gpr, loc,
):
    dp, tensor = lax.axis_index("dp"), lax.axis_index("tensor")
    x, h = dp // 2, dp % 2
    y, l, c = tensor // 8, (tensor // 2) % 4, tensor % 2
    chip = y * 4 + l

    def dev(x_, h_, y_, l_, c_):
        return (x_ * 2 + h_, y_ * 8 + l_ * 2 + c_)

    def mod4(v):
        return lax.rem(v, 4)

    sib = dev(x, h, y, l, 1 - c)
    yat = [dev(x, h, mod4(y + o), l, c) for o in range(4)]
    zat = [dev(x, h, y, mod4(l + o), c) for o in range(4)]
    xat = [dev(mod4(x + o), h, y, l, c) for o in range(4)]
    opposite = dev(x, 1 - h, y, l, c)
    dpat = [(lax.rem(dp + o, 8), tensor) for o in range(8)]
    crossing = lax.rem(l // 2 + h, 2)

    sends = []

    def copy(src, dst, send, recv, to):
        return pltpu.make_async_remote_copy(
            src_ref=src, dst_ref=dst, send_sem=send, recv_sem=recv, device_id=to, device_id_type=MESH
        )

    def put(src, dst, send, recv, to):
        made = copy(src, dst, send, recv, to)
        made.start()
        sends.append(made)

    def got(dst, recv):
        copy(dst, dst, recv, recv, sib).wait_recv()

    barrier = pltpu.get_barrier_semaphore()
    for to in [sib] + yat[1:] + zat[1:] + dpat[1:] + [dev(y, 1 - h, x, 2 * h + lax.rem(l, 2), c)]:
        pl.semaphore_signal(barrier, inc=1, device_id=to, device_id_type=MESH)

    own_x = pltpu.make_async_copy(x_in, XG.at[0, chip, c], loc.at[0])
    own_g = pltpu.make_async_copy(g_in, XG.at[1, chip, c], loc.at[1])
    load_wi = pltpu.make_async_copy(w_in, WI, loc.at[2])
    own_x.start()
    own_g.start()
    load_wi.start()

    def load_wo(j):
        return pltpu.make_async_copy(w_out.at[:, pl.ds(j * CHIP, CHIP)], WO.at[j], loc.at[3 + j])

    for j in range(16):
        load_wo(j).start()
    own_x.wait()
    own_g.wait()
    pl.semaphore_wait(barrier, 14 + 2 * crossing)

    def ring(n, ready, view, half, plus, minus, ss, rs, other=None):
        def first(i):
            ready(i)
            put(view(i, 0), view(i, 0), ss.at[i, 0], rs.at[i, 1], plus)
            put(view(i, 0), view(i, 0), ss.at[i, 1], rs.at[i, 0], minus)
            if other:
                put(view(i, 0), view(i, 0), ss.at[i, 4], rs.at[i, 4], sib)

        def second(i):
            got(view(i, 1), rs.at[i, 0])
            put(half(i, 1, 1), half(i, 1, 1), ss.at[i, 3], rs.at[i, 3], minus)
            got(view(i, 3), rs.at[i, 1])
            put(half(i, 3, 0), half(i, 3, 0), ss.at[i, 2], rs.at[i, 2], plus)
            if other:
                put(view(i, 1), view(i, 1), ss.at[i, 5], rs.at[i, 5], sib)
                put(view(i, 3), view(i, 3), ss.at[i, 7], rs.at[i, 7], sib)

        def third(i):
            got(half(i, 2, 0), rs.at[i, 2])
            got(half(i, 2, 1), rs.at[i, 3])
            if other:
                put(view(i, 2), view(i, 2), ss.at[i, 6], rs.at[i, 6], sib)

        def last(i):
            if other:
                for o in (0, 1, 3, 2):
                    got(other(i, o), rs.at[i, 4 + o])

        for t in range(n + 3):
            if t < n:
                first(t)
            if 0 <= t - 1 < n:
                second(t - 1)
            if 0 <= t - 2 < n:
                third(t - 2)
            if 0 <= t - 3 < n:
                last(t - 3)
                yield t - 3
            else:
                yield None

    def chip_at(i, o):
        return mod4(y + o) * 4 + mod4(l + i)

    def gather(a):
        def ready(i):
            if i > 0:
                got(XG.at[a, chip_at(i, 0), c], zr.at[a, i])

        return ring(
            4, ready,
            lambda i, o: XG.at[a, chip_at(i, o), c],
            lambda i, o, q: XG.at[a, chip_at(i, o), c, q],
            yat[1], yat[3], as_.at[a], ar.at[a],
            lambda i, o: XG.at[a, chip_at(i, o), 1 - c],
        )

    def slice_at(i, o, c_):
        lp = mod4(l + i)
        return (lp // 2, 2 * (2 * mod4(y + o) + (1 - h)) + lax.rem(lp, 2), c_)

    def slices():
        def ready(i):
            if i > 0:
                got(XS.at[slice_at(i, 0, c)], z2r.at[i])

        return ring(
            4, ready,
            lambda i, o: XS.at[slice_at(i, o, c)],
            lambda i, o, q: XS.at[slice_at(i, o, c) + (q,)],
            yat[1], yat[3], a2s, a2r,
            lambda i, o: XS.at[slice_at(i, o, 1 - c)],
        )

    def hidden_ring(a):
        def at(i, o):
            return (a, 2 * mod4(x + o) + (h if i == 0 else 1 - h))

        def ready(i):
            if i > 0:
                got(HB.at[at(1, 0)], z4r.at[a])

        return ring(
            2, ready,
            lambda i, o: HB.at[at(i, o)],
            lambda i, o, q: HB.at[at(i, o) + (q,)],
            xat[1], xat[3], hs.at[a], hr.at[a],
        )

    gx, gg = gather(0), gather(1)
    for a in range(2):
        for k in (1, 2, 3):
            put(XG.at[a, chip, c], XG.at[a, chip, c], zs.at[a, k], zr.at[a, k], zat[4 - k])
        if a == 0:
            next(gx)

    def cross(a):
        mine = XG.at[a, chip, c]
        there = XS.at[a, 2 * dp + lax.rem(l, 2), c]
        return copy(mine, there, ps.at[a], pr, dev(y, 1 - h, x, 2 * a + lax.rem(l, 2), c))

    @pl.when(crossing == 1)
    def _():
        cross(0).start()
        cross(1).start()

    def turn_gain(j, _):
        row = jnp.broadcast_to(gain[pl.ds(j, 1), :], (128, 128))
        GB[j // 3, pl.ds(pl.multiple_of(lax.rem(j, 3) * 128, 128), 128), :] = row.T
        return 0

    lax.fori_loop(0, 48, turn_gain, 0)
    load_wi.wait()

    def turn(j, _):
        WT[j] = WI[j].T.reshape(2, 2, 96, HID)
        return 0

    def stats(i):
        def one(o, _):
            j = mod4(y + o) * 4 + mod4(l + i)
            v = XG[0, j].reshape(CHIP, TOK).astype(F32)
            m = jnp.sum(v, axis=0, keepdims=True) * (1.0 / CHIP)
            e = v - m
            SM[pl.ds(4 * i + o, 1), :] = m
            SV[pl.ds(4 * i + o, 1), :] = jnp.sum(e * e, axis=0, keepdims=True)
            return 0

        lax.fori_loop(0, 4, one, 0)

    for t in range(6):
        if t < 4:
            lax.fori_loop(4 * t, 4 * t + 4, turn, 0)
        i = next(gx)
        if i is not None:
            stats(i)

    def exchange(a):
        for b in range(2):
            for o in (1, 3, 2):
                put(
                    XG.at[a, mod4(x + o) * 4 + 2 * h + b, c], XS.at[a, 2 * dp + b, c],
                    xs.at[a, b, o], xr.at[a, b, o], xat[o],
                )

    def own_slice(a):
        return pltpu.make_async_copy(
            XG.at[a, pl.ds(x * 4 + 2 * h, 2)], XS.at[a, pl.ds(2 * dp, 2)], loc.at[19 + a]
        )

    exchange(0)
    own_slice(0).start()
    next(gg)
    means = SM[...]
    mean = jnp.sum(means, axis=0, keepdims=True) * (1.0 / 16)
    off = means - mean
    spread = jnp.sum(SV[...], axis=0, keepdims=True) + CHIP * jnp.sum(off * off, axis=0, keepdims=True)
    inv = lax.rsqrt(spread * (1.0 / D) + 1e-06)
    ST[dp] = jnp.where(lax.broadcasted_iota(jnp.int32, (8, TOK), 0) == 0, mean, inv)
    for o in range(1, 8):
        put(ST.at[dp], ST.at[dp], sts.at[o], str_.at[o], dpat[o])

    def normalise(v, m, r, j):
        return ((v.astype(F32) - m) * r * wide(GB[j])).astype(BF16)

    PRE[...] = jnp.zeros_like(PRE)

    def pre_step(j, _):
        normed = normalise(XG[0, j].reshape(CHIP, TOK), ST[dp, 0:1, :], ST[dp, 1:2, :], j)
        PRE[...] += dot(WT[j].reshape(HID, CHIP), normed)
        return 0

    lax.fori_loop(0, 8, pre_step, 0)
    next(gg)
    lax.fori_loop(8, 16, pre_step, 0)

    pre = PRE[...]
    tanh = jnp.tanh(COEF * (pre + 0.044715 * pre * pre * pre))
    HB[0, dp] = (0.5 * pre * (1.0 + tanh)).astype(BF16).reshape(2, 192, TOK)
    PRE[...] = 0.5 * (1.0 + tanh) + 0.5 * pre * (1.0 - tanh * tanh) * COEF * (1.0 + 3.0 * 0.044715 * pre * pre)

    def over(a):
        put(HB.at[a, dp], HB.at[a, dp], z4s.at[a], z4r.at[a], opposite)

    over(0)
    ha, hg, sl = hidden_ring(0), hidden_ring(1), slices()
    next(ha)

    ACT[...] = jnp.zeros_like(ACT)
    for j in range(16):
        load_wo(j).wait()

    got(XS.at[slice_at(0, 0, c)], pr)
    for k in (1, 2, 3):
        put(XS.at[slice_at(0, 0, c)], XS.at[slice_at(0, 0, c)], z2s.at[k], z2r.at[k], zat[4 - k])

    for t in range(5):
        i = next(gg)
        if i is not None:
            def act_step(o, _):
                j = mod4(y + o) * 4 + mod4(l + i)
                ACT[...] += dot(WO[j], XG[1, j].reshape(CHIP, TOK))
                return 0

            lax.fori_loop(0, 4, act_step, 0)

    HB[1, dp] = (ACT[...] * PRE[...]).astype(BF16).reshape(2, 192, TOK)
    over(1)
    next(hg)
    exchange(1)
    own_slice(1).start()

    def partial(o):
        def one(q, _):
            j = mod4(y + o) * 4 + q
            part = dot(WI[j], HB[1, dp].reshape(HID, TOK))
            WT[j] = part.astype(BF16).reshape(2, 2, 96, TOK)
            copy(WT.at[j, 1 - c], R1.at[j], r1s.at[o, q], r1r.at[o, q], sib).start()
            return 0

        lax.fori_loop(0, 4, one, 0)

    def both(j, o, q):
        got(R1.at[j], r1r.at[o, q])
        return WT[j, c].astype(F32) + R1[j].astype(F32)

    for o in (2, 1, 3, 0):
        partial(o)
    next(ha)

    def far(q, _):
        j = mod4(y + 2) * 4 + q
        WT[j, c] = both(j, 2, q).astype(BF16)
        copy(WT.at[j, c, 0], R2.at[0, q], r2s.at[0, q], r2r.at[0, q], yat[1]).start()
        copy(WT.at[j, c, 1], R2.at[1, q], r2s.at[1, q], r2r.at[1, q], yat[3]).start()
        return 0

    lax.fori_loop(0, 4, far, 0)
    next(sl)

    def near(q, _):
        for o, w in ((1, 0), (3, 1)):
            j = mod4(y + o) * 4 + q
            total = both(j, o, q)
            got(R2.at[w, q], r2r.at[w, q])
            WT[j, c, w] = (total[w] + R2[w, q].astype(F32)).astype(BF16)
            WT[j, c, 1 - w] = total[1 - w].astype(BF16)
            copy(WT.at[j, c], R3.at[w, q], r3s.at[w, q], r3r.at[w, q], yat[o]).start()
        return 0

    lax.fori_loop(0, 4, near, 0)
    next(sl)
    next(hg)
    next(ha)

    def collect(k):
        q = mod4(l + k)
        j = y * 4 + q
        got(R3.at[0, q], r3r.at[0, q])
        got(R3.at[1, q], r3r.at[1, q])
        return both(j, 0, q) + R3[0, q].astype(F32) + R3[1, q].astype(F32)

    for k in (1, 2, 3):
        j = y * 4 + mod4(l + k)
        WT[j, c] = collect(k).astype(BF16)
        put(WT.at[j, c], R4.at[k], r4s.at[k], r4r.at[k], zat[k])
    TS[...] = collect(0)
    next(sl)
    next(hg)
    next(ha)
    for k in (1, 2, 3):
        got(R4.at[k], r4r.at[k])

    ng = TS[...] + R4[1].astype(F32) + R4[2].astype(F32) + R4[3].astype(F32) + attn[...].astype(F32)
    ng = ng.reshape(ROWS, TOK)
    own_gain = wide(GB[chip, pl.ds(pl.multiple_of(c * ROWS, ROWS), ROWS), :])
    xhat = (XG[0, chip, c].reshape(ROWS, TOK).astype(F32) - ST[dp, 0:1, :]) * ST[dp, 1:2, :]
    scaled = ng * own_gain
    s1 = jnp.sum(scaled, axis=0, keepdims=True)
    s2 = jnp.sum(scaled * xhat, axis=0, keepdims=True)
    MO[0] = jnp.where(lax.broadcasted_iota(jnp.int32, (8, TOK), 0) == 0, s1, s2)
    put(MO.at[0], MO.at[1], mos.at[0], mor.at[0], sib)
    prod = ng * xhat
    prod = prod[:, 0:128] + prod[:, 128:256] + prod[:, 256:384]
    prod = jnp.concatenate([prod, jnp.zeros((64, 128), F32)], axis=0).T
    GP[dp] = jnp.broadcast_to(jnp.sum(prod, axis=0, keepdims=True), (8, 256))
    for o in range(1, 8):
        put(GP.at[dp], GP.at[dp], gps.at[o], gpr.at[o], dpat[o])
    got(MO.at[1], mor.at[0])
    MO[2] = MO[0] + MO[1]
    for o in (1, 2, 3):
        put(MO.at[2], MO.at[2 + o], mos.at[o], mor.at[o], yat[o])
    next(sl)
    next(hg)
    for o in (1, 2, 3):
        got(MO.at[2 + o], mor.at[o])
    MO[6] = MO[2] + MO[3] + MO[4] + MO[5]
    for o in (1, 2, 3):
        put(MO.at[6], MO.at[6 + o], mos.at[3 + o], mor.at[3 + o], zat[o])

    for a in range(2):
        for b in range(2):
            for o in (1, 3, 2):
                at = XS.at[a, 2 * (2 * mod4(x + 4 - o) + h) + b, c]
                got(at, xr.at[a, b, o])
                put(at, at, xbs.at[a, b, o], xbr.at[a, b, o], sib)

    for o in (1, 2, 3):
        got(MO.at[6 + o], mor.at[3 + o])
    sums = (MO[6] + MO[7] + MO[8] + MO[9]) * (1.0 / D)
    xhat = (XG[0, chip, c].reshape(ROWS, TOK).astype(F32) - ST[dp, 0:1, :]) * ST[dp, 1:2, :]
    dx_out[...] = (
        XG[1, chip, c].reshape(ROWS, TOK).astype(F32)
        + (scaled - sums[0:1, :] - xhat * sums[1:2, :]) * ST[dp, 1:2, :]
    ).astype(BF16)

    for o in range(1, 8):
        got(GP.at[lax.rem(dp + 8 - o, 8)], gpr.at[o])
    total = GP[0]
    for o in range(1, 8):
        total = total + GP[o]
    gg_out[...] = total[0:1, 0:ROWS]

    for o in range(1, 8):
        got(ST.at[lax.rem(dp + 8 - o, 8)], str_.at[o])
    for a in range(2):
        own_slice(a).wait()
        for b in range(2):
            for o in (1, 3, 2):
                got(XS.at[a, 2 * (2 * mod4(x + 4 - o) + h) + b, 1 - c], xbr.at[a, b, o])

    dwin_out[...] = jnp.zeros_like(dwin_out)
    dwout_out[...] = jnp.zeros_like(dwout_out)

    def norm_of(d):
        for b in range(2):
            XN[2 * d + b] = normalise(
                XS[0, 2 * d + b].reshape(CHIP, TOK), ST[d, 0:1, :], ST[d, 1:2, :], 2 * dp + b
            )

    def half_sum(hh):
        def one(o, _):
            d = 2 * mod4(x + o) + hh
            norm_of(d)
            for b in range(2):
                dwin_out[pl.ds(b * CHIP, CHIP), :] += dot_nt(XN[2 * d + b], HB[1, d].reshape(HID, TOK))
                dwout_out[:, pl.ds(b * CHIP, CHIP)] += dot_nt(
                    HB[0, d].reshape(HID, TOK), XS[1, 2 * d + b].reshape(CHIP, TOK)
                )
            return 0

        lax.fori_loop(0, 4, one, 0)

    for g in (ha, hg):
        for _ in g:
            pass
    half_sum(h)
    for _ in sl:
        pass
    half_sum(1 - h)

    for made in sends:
        made.wait_send()

    @pl.when(crossing == 1)
    def _():
        cross(0).wait_send()
        cross(1).wait_send()

    def left(q, _):
        for o in range(4):
            j = mod4(y + o) * 4 + q
            copy(WT.at[j, 1 - c], R1.at[j], r1s.at[o, q], r1r.at[o, q], sib).wait_send()
        j = mod4(y + 2) * 4 + q
        copy(WT.at[j, c, 0], R2.at[0, q], r2s.at[0, q], r2r.at[0, q], yat[1]).wait_send()
        copy(WT.at[j, c, 1], R2.at[1, q], r2s.at[1, q], r2r.at[1, q], yat[3]).wait_send()
        for o, w in ((1, 0), (3, 1)):
            j = mod4(y + o) * 4 + q
            copy(WT.at[j, c], R3.at[w, q], r3s.at[w, q], r3r.at[w, q], yat[o]).wait_send()
        return 0

    lax.fori_loop(0, 4, left, 0)


def on_device(block_input, output_gradient, attn_grad, layernorm_gain, w_in, w_out):
    vmem, anywhere = pl.BlockSpec(memory_space=pltpu.VMEM), pl.BlockSpec(memory_space=pl.ANY)
    dma = pltpu.SemaphoreType.DMA
    pair = lambda *shape: [dma(shape), dma(shape)]
    scratch = [
        pltpu.VMEM((2, 16, 2, 2, 96, TOK), BF16),
        pltpu.VMEM((2, 16, 2, 2, 96, TOK), BF16),
        pltpu.VMEM((16, CHIP, TOK), BF16),
        pltpu.VMEM((16, CHIP, HID), BF16),
        pltpu.VMEM((16, 2, 2, 96, TOK), BF16),
        pltpu.VMEM((16, HID, CHIP), BF16),
        pltpu.VMEM((2, 8, 2, 192, TOK), BF16),
        pltpu.VMEM((16, CHIP, 128), F32),
        pltpu.VMEM((HID, TOK), F32),
        pltpu.VMEM((HID, TOK), F32),
        pltpu.VMEM((16, TOK), F32),
        pltpu.VMEM((16, TOK), F32),
        pltpu.VMEM((8, 8, TOK), F32),
        pltpu.VMEM((16, 2, 96, TOK), BF16),
        pltpu.VMEM((2, 4, 96, TOK), BF16),
        pltpu.VMEM((2, 4, 2, 96, TOK), BF16),
        pltpu.VMEM((4, 2, 96, TOK), BF16),
        pltpu.VMEM((2, 96, TOK), F32),
        pltpu.VMEM((10, 8, TOK), F32),
        pltpu.VMEM((8, 8, 256), F32),
    ]
    scratch += pair(2, 4) + pair(2, 4, 8) + pair(4) + pair(4, 8) + [dma((2,)), dma]
    scratch += pair(2, 2, 4) + pair(2) + pair(2, 2, 4) + pair(2, 2, 4)
    scratch += pair(4, 4) + pair(2, 4) + pair(2, 4) + pair(4) + pair(8) + pair(7) + pair(8) + [dma((21,))]
    dx, dgain, dw_in, dw_out = pl.pallas_call(
        kernel,
        out_shape=(
            jax.ShapeDtypeStruct((ROWS, TOK), BF16),
            jax.ShapeDtypeStruct((1, ROWS), F32),
            jax.ShapeDtypeStruct((768, HID), F32),
            jax.ShapeDtypeStruct((HID, 768), F32),
        ),
        in_specs=[anywhere, anywhere, vmem, vmem, anywhere, anywhere],
        out_specs=(vmem,) * 4,
        scratch_shapes=scratch,
        compiler_params=pltpu.CompilerParams(
            collective_id=0, has_side_effects=True, vmem_limit_bytes=62 * 2**20
        ),
        cost_estimate=pl.CostEstimate(flops=9 * 10**9, bytes_accessed=12 * 10**6, transcendentals=147456),
        name="parallel_block_backward",
    )(
        block_input.T.reshape(2, 96, TOK),
        output_gradient.T.reshape(2, 96, TOK),
        attn_grad.T.reshape(2, 96, TOK),
        layernorm_gain.reshape(48, 128),
        w_in.reshape(16, CHIP, HID),
        w_out,
    )
    return dx.T, dgain.reshape(ROWS), dw_in, dw_out


def solution(mesh):
    token = P("dp", "tensor")
    return jax.shard_map(
        on_device,
        mesh=mesh,
        in_specs=(token, token, token, P(), P(None, "tensor"), P("tensor", None)),
        out_specs=(token, P("tensor"), P("dp", "tensor"), P("tensor", "dp")),
        check_vma=False,
    )
```

```python
import functools
import math

import jax
import jax.numpy as jnp
from jax import lax
from jax.experimental import pallas as pl
from jax.experimental.pallas import tpu as pltpu
from jax.sharding import PartitionSpec as P

MESH = pl.DeviceIdType.MESH
F32, BF16 = jnp.float32, jnp.bfloat16
COEF = math.sqrt(2.0 / math.pi)
TOK = 384
HID = 384
ROWS = 192
CHIP = 384
D = 6144

NT = (((1,), (1,)), ((), ()))


def dot(a, b):
    return jnp.dot(a, b, preferred_element_type=F32)


def dot_nt(a, b):
    return lax.dot_general(a, b, NT, preferred_element_type=F32)


def wide(column):
    return jnp.concatenate([column] * (TOK // 128), axis=1)


def kernel(
    x_in, g_in, attn, gain, w_in, w_out,
    dx_out, gg_out, dwin_out, dwout_out,
    XG, XS, XN, WI, WT, WO, HB, GB, PRE, ACT, SL, WG, SM, SV, ST, R1, R2, R3, R4, TS, MO, GP,
    zs, zr, as_, ar, z2s, z2r, a2s, a2r, ps, pr, hs, hr, z4s, z4r, xs, xr, xbs, xbr, half_in, line_in, x_in_, y_in_,
    r1s, r1r, r2s, r2r, r3s, r3r, r4s, r4r, sts, str_, mos, mor, gps, gpr, loc,
):
    dp, tensor = lax.axis_index("dp"), lax.axis_index("tensor")
    x, h = dp // 2, dp % 2
    y, l, c = tensor // 8, (tensor // 2) % 4, tensor % 2
    chip = y * 4 + l

    def dev(x_, h_, y_, l_, c_):
        return (x_ * 2 + h_, y_ * 8 + l_ * 2 + c_)

    def mod4(v):
        return lax.rem(v, 4)

    sib = dev(x, h, y, l, 1 - c)
    yat = [dev(x, h, mod4(y + o), l, c) for o in range(4)]
    zat = [dev(x, h, y, mod4(l + o), c) for o in range(4)]
    xat = [dev(mod4(x + o), h, y, l, c) for o in range(4)]
    opposite = dev(x, 1 - h, y, l, c)
    dpat = [(lax.rem(dp + o, 8), tensor) for o in range(8)]
    crossing = lax.rem(l // 2 + h, 2)

    sends = []

    def copy(src, dst, send, recv, to):
        return pltpu.make_async_remote_copy(
            src_ref=src, dst_ref=dst, send_sem=send, recv_sem=recv, device_id=to, device_id_type=MESH
        )

    def put(src, dst, send, recv, to):
        made = copy(src, dst, send, recv, to)
        made.start()
        sends.append(made)

    def got(dst, recv):
        copy(dst, dst, recv, recv, sib).wait_recv()

    barrier = pltpu.get_barrier_semaphore()
    for to in [sib] + yat[1:] + zat[1:] + xat[1:]:
        pl.semaphore_signal(barrier, inc=1, device_id=to, device_id_type=MESH)

    @pl.when(l == 0)
    def _():
        pl.semaphore_signal(barrier, inc=1, device_id=dev(x, 1 - h, y, 3, c), device_id_type=MESH)

    @pl.when(l == 3)
    def _():
        pl.semaphore_signal(barrier, inc=1, device_id=dev(x, 1 - h, y, 0, c), device_id_type=MESH)

    own_x = pltpu.make_async_copy(x_in, XG.at[0, chip, c], loc.at[0])
    own_g = pltpu.make_async_copy(g_in, XG.at[1, chip, c], loc.at[1])
    load_wi = pltpu.make_async_copy(w_in, WI, loc.at[2])
    own_x.start()
    own_g.start()
    load_wi.start()

    def load_wo(j):
        return pltpu.make_async_copy(w_out.at[:, pl.ds(j * CHIP, CHIP)], WO.at[j], loc.at[3 + j])

    for j in range(16):
        load_wo(j).start()
    own_x.wait()
    own_g.wait()
    pl.semaphore_wait(barrier, jnp.where(lax.rem(l, 3) == 0, 11, 10))

    @pl.when(l == 0)
    def _():
        pl.semaphore_signal(half_in, inc=1, device_id=dev(x, 1 - h, y, 3, c), device_id_type=MESH)

    def pass_on(step):
        if step == 0:
            @pl.when(l == 3)
            def _():
                pl.semaphore_wait(half_in, 1)
                for to in zat[1:]:
                    pl.semaphore_signal(line_in, inc=1, device_id=to, device_id_type=MESH)
        if step == 1:
            @pl.when(l < 3)
            def _():
                pl.semaphore_wait(line_in, 1)

            for to in xat[1:]:
                pl.semaphore_signal(x_in_, inc=1, device_id=to, device_id_type=MESH)
        if step == 2:
            pl.semaphore_wait(x_in_, 3)
            for to in yat[1:]:
                pl.semaphore_signal(y_in_, inc=1, device_id=to, device_id_type=MESH)
        if step == 3:
            pl.semaphore_wait(y_in_, 3)

    def ring(n, ready, view, half, plus, minus, ss, rs, other=None):
        def first(i):
            ready(i)
            put(view(i, 0), view(i, 0), ss.at[i, 0], rs.at[i, 1], plus)
            put(view(i, 0), view(i, 0), ss.at[i, 1], rs.at[i, 0], minus)
            if other:
                put(view(i, 0), view(i, 0), ss.at[i, 4], rs.at[i, 4], sib)

        def second(i):
            got(view(i, 1), rs.at[i, 0])
            put(half(i, 1, 1), half(i, 1, 1), ss.at[i, 3], rs.at[i, 3], minus)
            got(view(i, 3), rs.at[i, 1])
            put(half(i, 3, 0), half(i, 3, 0), ss.at[i, 2], rs.at[i, 2], plus)
            if other:
                put(view(i, 1), view(i, 1), ss.at[i, 5], rs.at[i, 5], sib)
                put(view(i, 3), view(i, 3), ss.at[i, 7], rs.at[i, 7], sib)

        def third(i):
            got(half(i, 2, 0), rs.at[i, 2])
            got(half(i, 2, 1), rs.at[i, 3])
            if other:
                put(view(i, 2), view(i, 2), ss.at[i, 6], rs.at[i, 6], sib)

        def last(i):
            if other:
                for o in (0, 1, 3, 2):
                    got(other(i, o), rs.at[i, 4 + o])

        for t in range(n + 3):
            if t < n and other:
                first(t)
                yield None
            if 0 <= t - 1 < n:
                second(t - 1)
                yield None
            if t < n and not other:
                first(t)
                yield None
            if 0 <= t - 2 < n:
                third(t - 2)
                yield None
            if 0 <= t - 3 < n:
                last(t - 3)
            yield t

    def chip_at(i, o):
        return mod4(y + o) * 4 + mod4(l + i)

    queue = [(a, k) for a in range(2) for k in (1, 2, 3)]

    def along_z(count):
        for a, k in queue[:count]:
            put(XG.at[a, chip, c], XG.at[a, chip, c], zs.at[a, k], zr.at[a, k], zat[4 - k])
        del queue[:count]

    order = [(0, 0), (1, 0), (0, 1), (0, 2), (0, 3), (1, 1), (1, 2), (1, 3)]

    def gather():
        def block(i, o, c_):
            a, k = order[i]
            return XG.at[a, chip_at(k, o), c_]

        def ready(i):
            a, k = order[i]
            if k > 0:
                got(block(i, 0, c), zr.at[a, k])
            if i > 0:
                along_z(1)

        return ring(
            8, ready,
            lambda i, o: block(i, o, c),
            lambda i, o, q: XG.at[order[i][0], chip_at(order[i][1], o), c, q],
            yat[1], yat[3], as_, ar,
            lambda i, o: block(i, o, 1 - c),
        )

    def slice_at(i, o, c_):
        lp = mod4(l + i)
        return (lp // 2, 2 * (2 * mod4(y + o) + (1 - h)) + lax.rem(lp, 2), c_)

    def slice_along_z(ks):
        for k in ks:
            put(XS.at[slice_at(0, 0, c)], XS.at[slice_at(0, 0, c)], z2s.at[k], z2r.at[k], zat[4 - k])

    def slices():
        def ready(i):
            if i > 0:
                got(XS.at[slice_at(i, 0, c)], z2r.at[i])
            if i == 1:
                slice_along_z((3,))

        return ring(
            4, ready,
            lambda i, o: XS.at[slice_at(i, o, c)],
            lambda i, o, q: XS.at[slice_at(i, o, c) + (q,)],
            yat[1], yat[3], a2s, a2r,
            lambda i, o: XS.at[slice_at(i, o, 1 - c)],
        )

    def hidden_ring(a):
        def at(i, o):
            return (a, 2 * mod4(x + o) + (h if i == 0 else 1 - h))

        def ready(i):
            if i > 0:
                got(HB.at[at(1, 0)], z4r.at[a])

        return ring(
            2, ready,
            lambda i, o: HB.at[at(i, o)],
            lambda i, o, q: HB.at[at(i, o) + (q,)],
            xat[1], xat[3], hs.at[a], hr.at[a],
        )

    tok = gather()
    def step(ring_, t, between=None):
        while True:
            at = next(ring_, t)
            if at == t:
                return
            if between is not None:
                between()

    along_z(2)
    step(tok, 0)

    def cross(a):
        mine = XG.at[a, chip, c]
        there = XS.at[a, 2 * dp + lax.rem(l, 2), c]
        return copy(mine, there, ps.at[a], pr, dev(y, 1 - h, x, 2 * a + lax.rem(l, 2), c))

    def cross_over():
        @pl.when(crossing == 1)
        def _():
            cross(0).start()
            cross(1).start()

    def turn_gain(j, _):
        row = jnp.broadcast_to(gain[pl.ds(j, 1), :], (128, 128))
        GB[j // 3, pl.ds(pl.multiple_of(lax.rem(j, 3) * 128, 128), 128), :] = row.T
        return 0

    load_wi.wait()

    def turn(j, _):
        WT[j] = WI[j].T.reshape(2, 2, 96, HID)
        return 0

    def stats(i):
        def one(o, _):
            j = mod4(y + o) * 4 + mod4(l + i)
            v = XG[0, j].reshape(CHIP, TOK).astype(F32)
            m = jnp.sum(v, axis=0, keepdims=True) * (1.0 / CHIP)
            e = v - m
            SM[pl.ds(4 * i + o, 1), :] = m
            SV[pl.ds(4 * i + o, 1), :] = jnp.sum(e * e, axis=0, keepdims=True)
            return 0

        lax.fori_loop(0, 4, one, 0, unroll=2)

    def share(a, i):
        lp = mod4(l + i)
        b = lax.rem(lp, 2)

        @pl.when(lp // 2 == h)
        def _():
            for o in (1, 3, 2):
                copy(
                    XG.at[a, mod4(x + o) * 4 + lp, c], XS.at[a, 2 * dp + b, c],
                    xs.at[a, b, o], xr.at[a, b, o], xat[o],
                ).start()

    def relay(a):
        for b in range(2):
            for o in (1, 3, 2):
                at = XS.at[a, 2 * (2 * mod4(x + 4 - o) + h) + b, c]
                got(at, xr.at[a, b, o])
                put(at, at, xbs.at[a, b, o], xbr.at[a, b, o], sib)

    def relayed(a):
        own_slice(a).wait()
        for b in range(2):
            for o in (1, 3, 2):
                got(XS.at[a, 2 * (2 * mod4(x + 4 - o) + h) + b, 1 - c], xbr.at[a, b, o])

    def own_slice(a):
        return pltpu.make_async_copy(
            XG.at[a, pl.ds(x * 4 + 2 * h, 2)], XS.at[a, pl.ds(2 * dp, 2)], loc.at[19 + a]
        )

    def gain_step(j, _):
        g = GB[j]
        high = g.astype(BF16)
        low = (g - high.astype(F32)).astype(BF16)
        w = WT[j].reshape(HID, CHIP)
        WG[...] += dot(w, high) + dot(w, low)
        return 0

    def act_step(i):
        def one(o, _):
            j = mod4(y + o) * 4 + mod4(l + i)
            ACT[...] += dot(WO[j], XG[1, j].reshape(CHIP, TOK))
            return 0

        lax.fori_loop(0, 4, one, 0, unroll=True)

    WG[...] = jnp.zeros_like(WG)
    ACT[...] = jnp.zeros_like(ACT)
    pass_on(0)
    lax.fori_loop(0, 8, turn, 0, unroll=2)
    pass_on(1)
    lax.fori_loop(0, 12, turn_gain, 0, unroll=4)
    step(tok, 1)
    pass_on(2)
    lax.fori_loop(8, 16, turn, 0, unroll=2)
    lax.fori_loop(12, 24, turn_gain, 0, unroll=4)
    step(tok, 2)
    share(0, 0)
    pass_on(3)
    cross_over()
    lax.fori_loop(24, 48, turn_gain, 0, unroll=4)
    step(tok, 3)
    share(1, 0)
    stats(0)
    step(tok, 4)
    share(0, 1)
    for j in range(16):
        load_wo(j).wait()
    lax.fori_loop(0, 8, gain_step, 0, unroll=2)
    step(tok, 5)
    share(0, 2)
    stats(1)
    lax.fori_loop(8, 16, gain_step, 0, unroll=2)
    step(tok, 6)
    share(0, 3)
    stats(2)
    act_step(0)
    step(tok, 7)
    share(1, 1)
    stats(3)

    own_slice(0).start()
    means = SM[...]
    mean = jnp.sum(means, axis=0, keepdims=True) * (1.0 / 16)
    off = means - mean
    spread = jnp.sum(SV[...], axis=0, keepdims=True) + CHIP * jnp.sum(off * off, axis=0, keepdims=True)
    inv = lax.rsqrt(spread * (1.0 / D) + 1e-06)
    ST[dp] = jnp.where(lax.broadcasted_iota(jnp.int32, (8, TOK), 0) == 0, mean, inv)
    for o in range(1, 8):
        put(ST.at[dp], ST.at[dp], sts.at[o], str_.at[o], dpat[o])

    def normalise(v, m, r, j):
        return ((v.astype(F32) - m) * r * wide(GB[j])).astype(BF16)

    PRE[...] = jnp.zeros_like(PRE)

    def pre_step(j, _):
        normed = normalise(XG[0, j].reshape(CHIP, TOK), ST[dp, 0:1, :], ST[dp, 1:2, :], j)
        PRE[...] += dot(WT[j].reshape(HID, CHIP), normed)
        return 0

    pieces = [lambda b=b: lax.fori_loop(4 * b, 4 * b + 4, pre_step, 0, unroll=True) for b in range(4)]

    def piece():
        if pieces:
            pieces.pop(0)()

    piece()
    step(tok, 8, piece)
    while pieces:
        piece()

    pre = PRE[...]
    tanh = jnp.tanh(COEF * (pre + 0.044715 * pre * pre * pre))
    HB[0, dp] = (0.5 * pre * (1.0 + tanh)).astype(BF16).reshape(2, 192, TOK)
    SL[...] = 0.5 * (1.0 + tanh) + 0.5 * pre * (1.0 - tanh * tanh) * COEF * (1.0 + 3.0 * 0.044715 * pre * pre)

    def over(a):
        put(HB.at[a, dp], HB.at[a, dp], z4s.at[a], z4r.at[a], opposite)

    over(0)
    ha, hg, sl = hidden_ring(0), hidden_ring(1), slices()
    step(ha, 0)
    share(1, 2)
    got(XS.at[slice_at(0, 0, c)], pr)
    slice_along_z((1, 2))
    act_step(1)
    step(tok, 9)
    share(1, 3)
    step(sl, 0)
    act_step(2)
    relay(0)
    step(tok, 10)
    act_step(3)

    HB[1, dp] = (ACT[...] * SL[...]).astype(BF16).reshape(2, 192, TOK)
    over(1)
    step(hg, 0)
    own_slice(1).start()

    own_gain = wide(GB[chip, pl.ds(pl.multiple_of(c * ROWS, ROWS), ROWS), :])

    def own_xhat():
        return (XG[0, chip, c].reshape(ROWS, TOK).astype(F32) - ST[dp, 0:1, :]) * ST[dp, 1:2, :]

    def row_sums():
        grad = HB[1, dp].reshape(HID, TOK).astype(F32)
        side = attn[...].reshape(ROWS, TOK).astype(F32) * own_gain
        s1 = jnp.sum(grad * wide(WG[...]), axis=0, keepdims=True) + jnp.sum(side, axis=0, keepdims=True)
        s2 = jnp.sum(grad * PRE[...], axis=0, keepdims=True) + jnp.sum(side * own_xhat(), axis=0, keepdims=True)
        MO[0] = jnp.where(lax.broadcasted_iota(jnp.int32, (8, TOK), 0) == 0, s1, s2)
        put(MO.at[0], MO.at[1], mos.at[0], mor.at[0], sib)

    def row_sums_y():
        got(MO.at[1], mor.at[0])
        MO[2] = MO[0] + MO[1]
        for o in (1, 2, 3):
            put(MO.at[2], MO.at[2 + o], mos.at[o], mor.at[o], yat[o])

    def row_sums_z():
        for o in (1, 2, 3):
            got(MO.at[2 + o], mor.at[o])
        MO[6] = MO[2] + MO[3] + MO[4] + MO[5]
        for o in (1, 2, 3):
            put(MO.at[6], MO.at[6 + o], mos.at[3 + o], mor.at[3 + o], zat[o])

    def partial(o):
        def one(n, _):
            q = mod4(l + 1 + n)
            j = mod4(y + o) * 4 + q
            part = dot(WI[j], HB[1, dp].reshape(HID, TOK))
            WT[j] = part.astype(BF16).reshape(2, 2, 96, TOK)
            copy(WT.at[j, 1 - c], R1.at[j], r1s.at[o, q], r1r.at[o, q], sib).start()
            return 0

        lax.fori_loop(0, 4, one, 0, unroll=True)

    def both(j, o, q):
        got(R1.at[j], r1r.at[o, q])
        return WT[j, c].astype(F32) + R1[j].astype(F32)

    partial(2)
    partial(1)
    def far(n, _):
        q = mod4(l + 1 + n)
        j = mod4(y + 2) * 4 + q
        WT[j, c] = both(j, 2, q).astype(BF16)
        copy(WT.at[j, c, 0], R2.at[0, q], r2s.at[0, q], r2r.at[0, q], yat[1]).start()
        copy(WT.at[j, c, 1], R2.at[1, q], r2s.at[1, q], r2r.at[1, q], yat[3]).start()
        return 0

    lax.fori_loop(0, 4, far, 0)
    partial(3)
    row_sums()
    partial(0)
    step(sl, 1)
    row_sums_y()

    def near(n, _):
        q = mod4(l + 1 + n)
        for o, w in ((1, 0), (3, 1)):
            j = mod4(y + o) * 4 + q
            total = both(j, o, q)
            got(R2.at[w, q], r2r.at[w, q])
            WT[j, c, w] = (total[w] + R2[w, q].astype(F32)).astype(BF16)
            WT[j, c, 1 - w] = total[1 - w].astype(BF16)
            copy(WT.at[j, c], R3.at[w, q], r3s.at[w, q], r3r.at[w, q], yat[o]).start()
        return 0

    lax.fori_loop(0, 4, near, 0)

    def norm_of(hh):
        def one(o, _):
            d = 2 * mod4(x + o) + hh
            for b in range(2):
                XN[2 * d + b] = normalise(
                    XS[0, 2 * d + b].reshape(CHIP, TOK), ST[d, 0:1, :], ST[d, 1:2, :], 2 * dp + b
                )
            return 0

        lax.fori_loop(0, 4, one, 0, unroll=2)

    def sum_in(hh):
        def one(o, _):
            d = 2 * mod4(x + o) + hh
            dwin_out[...] += dot_nt(XN[pl.ds(2 * d, 2)].reshape(768, TOK), HB[1, d].reshape(HID, TOK))
            return 0

        lax.fori_loop(0, 4, one, 0, unroll=2)

    def sum_out(hh):
        def one(o, _):
            d = 2 * mod4(x + o) + hh
            dwout_out[...] += dot_nt(HB[0, d].reshape(HID, TOK), XS[1, pl.ds(2 * d, 2)].reshape(768, TOK))
            return 0

        lax.fori_loop(0, 4, one, 0, unroll=2)

    dwin_out[...] = jnp.zeros_like(dwin_out)
    dwout_out[...] = jnp.zeros_like(dwout_out)
    step(ha, 1)
    row_sums_z()
    relay(1)
    step(ha, 2)
    step(sl, 2)
    step(hg, 1)
    for o in range(1, 8):
        got(ST.at[lax.rem(dp + 8 - o, 8)], str_.at[o])
    relayed(0)
    norm_of(h)
    relayed(1)
    sum_out(h)

    def collect(k):
        q = mod4(l + k)
        j = y * 4 + q
        got(R3.at[0, q], r3r.at[0, q])
        got(R3.at[1, q], r3r.at[1, q])
        return both(j, 0, q) + R3[0, q].astype(F32) + R3[1, q].astype(F32)

    for k in (1, 2, 3):
        j = y * 4 + mod4(l + k)
        WT[j, c] = collect(k).astype(BF16)
        put(WT.at[j, c], R4.at[k], r4s.at[k], r4r.at[k], zat[k])
    TS[...] = collect(0)
    step(sl, 3)
    step(hg, 2)
    for k in (1, 2, 3):
        got(R4.at[k], r4r.at[k])

    ng = TS[...] + R4[1].astype(F32) + R4[2].astype(F32) + R4[3].astype(F32) + attn[...].astype(F32)
    ng = ng.reshape(ROWS, TOK)
    xhat = own_xhat()
    prod = ng * xhat
    prod = prod[:, 0:128] + prod[:, 128:256] + prod[:, 256:384]
    prod = jnp.concatenate([prod, jnp.zeros((64, 128), F32)], axis=0).T
    GP[dp] = jnp.broadcast_to(jnp.sum(prod, axis=0, keepdims=True), (8, 256))
    for o in range(1, 8):
        put(GP.at[dp], GP.at[dp], gps.at[o], gpr.at[o], dpat[o])
    step(sl, 4)
    for o in (1, 2, 3):
        got(MO.at[6 + o], mor.at[3 + o])
    sums = (MO[6] + MO[7] + MO[8] + MO[9]) * (1.0 / D)
    dx_out[...] = (
        XG[1, chip, c].reshape(ROWS, TOK).astype(F32)
        + (ng * own_gain - sums[0:1, :] - xhat * sums[1:2, :]) * ST[dp, 1:2, :]
    ).astype(BF16)
    sum_in(h)
    for g in (ha, hg, sl):
        for _ in g:
            pass
    sum_out(1 - h)
    norm_of(1 - h)
    sum_in(1 - h)

    for o in range(1, 8):
        got(GP.at[lax.rem(dp + 8 - o, 8)], gpr.at[o])
    total = GP[0]
    for o in range(1, 8):
        total = total + GP[o]
    gg_out[...] = total[0:1, 0:ROWS]

    for made in sends:
        made.wait_send()
    for a in range(2):
        for b in range(2):
            for o in (1, 2, 3):
                copy(
                    XG.at[a, mod4(x + o) * 4 + 2 * h + b, c], XS.at[a, 2 * dp + b, c],
                    xs.at[a, b, o], xr.at[a, b, o], xat[o],
                ).wait_send()

    @pl.when(crossing == 1)
    def _():
        cross(0).wait_send()
        cross(1).wait_send()

    def left(q, _):
        for o in range(4):
            j = mod4(y + o) * 4 + q
            copy(WT.at[j, 1 - c], R1.at[j], r1s.at[o, q], r1r.at[o, q], sib).wait_send()
        j = mod4(y + 2) * 4 + q
        copy(WT.at[j, c, 0], R2.at[0, q], r2s.at[0, q], r2r.at[0, q], yat[1]).wait_send()
        copy(WT.at[j, c, 1], R2.at[1, q], r2s.at[1, q], r2r.at[1, q], yat[3]).wait_send()
        for o, w in ((1, 0), (3, 1)):
            j = mod4(y + o) * 4 + q
            copy(WT.at[j, c], R3.at[w, q], r3s.at[w, q], r3r.at[w, q], yat[o]).wait_send()
        return 0

    lax.fori_loop(0, 4, left, 0)


def hand_over(*refs):
    sources, results, between, sems = refs[:4], refs[4:8], refs[8:12], refs[12]
    arrive = [pltpu.make_async_copy(a, b, sems.at[0, i]) for i, (a, b) in enumerate(zip(sources, between))]
    leave = [pltpu.make_async_copy(a, b, sems.at[1, i]) for i, (a, b) in enumerate(zip(between, results))]
    for made in arrive:
        made.start()
    for one, two in zip(arrive, leave):
        one.wait()
        two.start()
    for made in leave:
        made.wait()


def on_device(block_input, output_gradient, attn_grad, layernorm_gain, w_in, w_out):
    vmem, anywhere = pl.BlockSpec(memory_space=pltpu.VMEM), pl.BlockSpec(memory_space=pl.ANY)
    dma = pltpu.SemaphoreType.DMA
    pair = lambda *shape: [dma(shape), dma(shape)]
    scratch = [
        pltpu.VMEM((2, 16, 2, 2, 96, TOK), BF16),
        pltpu.VMEM((2, 16, 2, 2, 96, TOK), BF16),
        pltpu.VMEM((16, CHIP, TOK), BF16),
        pltpu.VMEM((16, CHIP, HID), BF16),
        pltpu.VMEM((16, 2, 2, 96, TOK), BF16),
        pltpu.VMEM((16, HID, CHIP), BF16),
        pltpu.VMEM((2, 8, 2, 192, TOK), BF16),
        pltpu.VMEM((16, CHIP, 128), F32),
        pltpu.VMEM((HID, TOK), F32),
        pltpu.VMEM((HID, TOK), F32),
        pltpu.VMEM((HID, TOK), F32),
        pltpu.VMEM((HID, 128), F32),
        pltpu.VMEM((16, TOK), F32),
        pltpu.VMEM((16, TOK), F32),
        pltpu.VMEM((8, 8, TOK), F32),
        pltpu.VMEM((16, 2, 96, TOK), BF16),
        pltpu.VMEM((2, 4, 96, TOK), BF16),
        pltpu.VMEM((2, 4, 2, 96, TOK), BF16),
        pltpu.VMEM((4, 2, 96, TOK), BF16),
        pltpu.VMEM((2, 96, TOK), F32),
        pltpu.VMEM((10, 8, TOK), F32),
        pltpu.VMEM((8, 8, 256), F32),
    ]
    scratch += pair(2, 4) + pair(8, 8) + pair(4) + pair(4, 8) + [dma((2,)), dma]
    scratch += pair(2, 2, 4) + pair(2) + pair(2, 2, 4) + pair(2, 2, 4)
    scratch += [pltpu.SemaphoreType.REGULAR] * 4
    scratch += pair(4, 4) + pair(2, 4) + pair(2, 4) + pair(4) + pair(8) + pair(7) + pair(8) + [dma((21,))]
    shapes = (
        jax.ShapeDtypeStruct((ROWS, TOK), BF16),
        jax.ShapeDtypeStruct((1, ROWS), F32),
        jax.ShapeDtypeStruct((768, HID), F32),
        jax.ShapeDtypeStruct((HID, 768), F32),
    )
    results = pl.pallas_call(
        kernel,
        out_shape=shapes,
        in_specs=[anywhere, anywhere, vmem, vmem, anywhere, anywhere],
        out_specs=(vmem,) * 4,
        scratch_shapes=scratch,
        compiler_params=pltpu.CompilerParams(
            collective_id=0, has_side_effects=True, vmem_limit_bytes=62 * 2**20
        ),
        cost_estimate=pl.CostEstimate(flops=9 * 10**9, bytes_accessed=12 * 10**6, transcendentals=147456),
        name="parallel_block_backward",
    )(
        block_input.T.reshape(2, 96, TOK),
        output_gradient.T.reshape(2, 96, TOK),
        attn_grad.T.reshape(2, 96, TOK),
        layernorm_gain.reshape(48, 128),
        w_in.reshape(16, CHIP, HID),
        w_out,
    )
    dx, dgain, dw_in, dw_out = pl.pallas_call(
        hand_over,
        out_shape=shapes,
        in_specs=[anywhere] * 4,
        out_specs=(anywhere,) * 4,
        scratch_shapes=[pltpu.VMEM(s.shape, s.dtype) for s in shapes] + [dma((2, 4))],
        name="results",
    )(*results)
    return dx.T, dgain.reshape(ROWS), dw_in, dw_out


def solution(mesh):
    token = P("dp", "tensor")
    return jax.shard_map(
        on_device,
        mesh=mesh,
        in_specs=(token, token, token, P(), P(None, "tensor"), P("tensor", None)),
        out_specs=(token, P("tensor"), P("dp", "tensor"), P("tensor", "dp")),
        check_vma=False,
    )
```

```python
import functools
import math

import jax
import jax.numpy as jnp
from jax import lax
from jax.experimental import pallas as pl
from jax.experimental.pallas import tpu as pltpu
from jax.sharding import PartitionSpec as P

MESH = pl.DeviceIdType.MESH
F32, BF16 = jnp.float32, jnp.bfloat16
COEF = math.sqrt(2.0 / math.pi)
TOK = 384
HID = 384
ROWS = 192
CHIP = 384
D = 6144

NT = (((1,), (1,)), ((), ()))


def dot(a, b):
    return jnp.dot(a, b, preferred_element_type=F32)


def dot_nt(a, b):
    return lax.dot_general(a, b, NT, preferred_element_type=F32)


def wide(column):
    return jnp.concatenate([column] * (TOK // 128), axis=1)


def kernel(
    x_in, g_in, attn, gain, w_in, w_out,
    dx_out, gg_out, dwin_out, dwout_out,
    XG, XS, XN, WI, WT, WO, HB, GB, PRE, ACT, SL, WG, SM, SV, ST, R1, R2, R3, R4, TS, MO, GP,
    zs, zr, as_, ar, z2s, z2r, a2s, a2r, ps, pr, hs, hr, z4s, z4r, xs, xr, xbs, xbr, half_in, line_in, x_in_, y_in_,
    r1s, r1r, r2s, r2r, r3s, r3r, r4s, r4r, sts, str_, mos, mor, gps, gpr, loc,
):
    dp, tensor = lax.axis_index("dp"), lax.axis_index("tensor")
    x, h = dp // 2, dp % 2
    y, l, c = tensor // 8, (tensor // 2) % 4, tensor % 2
    chip = y * 4 + l

    def dev(x_, h_, y_, l_, c_):
        return (x_ * 2 + h_, y_ * 8 + l_ * 2 + c_)

    def mod4(v):
        return lax.rem(v, 4)

    sib = dev(x, h, y, l, 1 - c)
    yat = [dev(x, h, mod4(y + o), l, c) for o in range(4)]
    zat = [dev(x, h, y, mod4(l + o), c) for o in range(4)]
    xat = [dev(mod4(x + o), h, y, l, c) for o in range(4)]
    opposite = dev(x, 1 - h, y, l, c)
    dpat = [(lax.rem(dp + o, 8), tensor) for o in range(8)]
    crossing = lax.rem(l // 2 + h, 2)

    sends = []

    def copy(src, dst, send, recv, to):
        return pltpu.make_async_remote_copy(
            src_ref=src, dst_ref=dst, send_sem=send, recv_sem=recv, device_id=to, device_id_type=MESH
        )

    def put(src, dst, send, recv, to):
        made = copy(src, dst, send, recv, to)
        made.start()
        sends.append(made)

    def got(dst, recv):
        copy(dst, dst, recv, recv, sib).wait_recv()

    barrier = pltpu.get_barrier_semaphore()
    for to in [sib] + yat[1:] + zat[1:] + xat[1:]:
        pl.semaphore_signal(barrier, inc=1, device_id=to, device_id_type=MESH)

    @pl.when(l == 0)
    def _():
        pl.semaphore_signal(barrier, inc=1, device_id=dev(x, 1 - h, y, 3, c), device_id_type=MESH)

    @pl.when(l == 3)
    def _():
        pl.semaphore_signal(barrier, inc=1, device_id=dev(x, 1 - h, y, 0, c), device_id_type=MESH)

    own_x = pltpu.make_async_copy(x_in, XG.at[0, chip, c], loc.at[0])
    own_g = pltpu.make_async_copy(g_in, XG.at[1, chip, c], loc.at[1])
    load_wi = pltpu.make_async_copy(w_in, WI, loc.at[2])
    own_x.start()
    own_g.start()
    load_wi.start()

    def load_wo(j):
        return pltpu.make_async_copy(w_out.at[:, pl.ds(j * CHIP, CHIP)], WO.at[j], loc.at[3 + j])

    for j in range(16):
        load_wo(j).start()
    own_x.wait()
    own_g.wait()
    pl.semaphore_wait(barrier, jnp.where(lax.rem(l, 3) == 0, 11, 10))

    @pl.when(l == 0)
    def _():
        pl.semaphore_signal(half_in, inc=1, device_id=dev(x, 1 - h, y, 3, c), device_id_type=MESH)

    def pass_on(step):
        if step == 0:
            @pl.when(l == 3)
            def _():
                pl.semaphore_wait(half_in, 1)
                for to in zat[1:]:
                    pl.semaphore_signal(line_in, inc=1, device_id=to, device_id_type=MESH)
        if step == 1:
            @pl.when(l < 3)
            def _():
                pl.semaphore_wait(line_in, 1)

            for to in xat[1:]:
                pl.semaphore_signal(x_in_, inc=1, device_id=to, device_id_type=MESH)
        if step == 2:
            pl.semaphore_wait(x_in_, 3)
            for to in yat[1:]:
                pl.semaphore_signal(y_in_, inc=1, device_id=to, device_id_type=MESH)
        if step == 3:
            pl.semaphore_wait(y_in_, 3)

    def ring(n, ready, view, half, plus, minus, ss, rs, other=None):
        def first(i):
            ready(i)
            put(view(i, 0), view(i, 0), ss.at[i, 0], rs.at[i, 1], plus)
            put(view(i, 0), view(i, 0), ss.at[i, 1], rs.at[i, 0], minus)
            if other:
                put(view(i, 0), view(i, 0), ss.at[i, 4], rs.at[i, 4], sib)

        def second(i):
            got(view(i, 1), rs.at[i, 0])
            put(half(i, 1, 1), half(i, 1, 1), ss.at[i, 3], rs.at[i, 3], minus)
            got(view(i, 3), rs.at[i, 1])
            put(half(i, 3, 0), half(i, 3, 0), ss.at[i, 2], rs.at[i, 2], plus)
            if other:
                put(view(i, 1), view(i, 1), ss.at[i, 5], rs.at[i, 5], sib)
                put(view(i, 3), view(i, 3), ss.at[i, 7], rs.at[i, 7], sib)

        def third(i):
            got(half(i, 2, 0), rs.at[i, 2])
            got(half(i, 2, 1), rs.at[i, 3])
            if other:
                put(view(i, 2), view(i, 2), ss.at[i, 6], rs.at[i, 6], sib)

        def last(i):
            if other:
                for o in (0, 1, 3, 2):
                    got(other(i, o), rs.at[i, 4 + o])

        for t in range(n + 3):
            if t < n and other:
                first(t)
                yield None
            if 0 <= t - 1 < n:
                second(t - 1)
                yield None
            if t < n and not other:
                first(t)
                yield None
            if 0 <= t - 2 < n:
                third(t - 2)
                yield None
            if 0 <= t - 3 < n:
                last(t - 3)
            yield t

    def chip_at(i, o):
        return mod4(y + o) * 4 + mod4(l + i)

    queue = [(a, k) for a in range(2) for k in (1, 2, 3)]

    def along_z(count):
        for a, k in queue[:count]:
            put(XG.at[a, chip, c], XG.at[a, chip, c], zs.at[a, k], zr.at[a, k], zat[4 - k])
        del queue[:count]

    order = [(a, k) for a in range(2) for k in range(4)]

    def gather():
        def block(i, o, c_):
            a, k = order[i]
            return XG.at[a, chip_at(k, o), c_]

        def ready(i):
            a, k = order[i]
            if k > 0:
                got(block(i, 0, c), zr.at[a, k])
            if i > 0:
                along_z(1)

        return ring(
            8, ready,
            lambda i, o: block(i, o, c),
            lambda i, o, q: XG.at[order[i][0], chip_at(order[i][1], o), c, q],
            yat[1], yat[3], as_, ar,
            lambda i, o: block(i, o, 1 - c),
        )

    def slice_at(i, o, c_):
        lp = mod4(l + i)
        return (lp // 2, 2 * (2 * mod4(y + o) + (1 - h)) + lax.rem(lp, 2), c_)

    def slice_along_z(ks):
        for k in ks:
            put(XS.at[slice_at(0, 0, c)], XS.at[slice_at(0, 0, c)], z2s.at[k], z2r.at[k], zat[4 - k])

    def slices():
        def ready(i):
            if i > 0:
                got(XS.at[slice_at(i, 0, c)], z2r.at[i])

        return ring(
            4, ready,
            lambda i, o: XS.at[slice_at(i, o, c)],
            lambda i, o, q: XS.at[slice_at(i, o, c) + (q,)],
            yat[1], yat[3], a2s, a2r,
            lambda i, o: XS.at[slice_at(i, o, 1 - c)],
        )

    def hidden_ring(a):
        def at(i, o):
            return (a, 2 * mod4(x + o) + (h if i == 0 else 1 - h))

        def ready(i):
            if i > 0:
                got(HB.at[at(1, 0)], z4r.at[a])

        return ring(
            2, ready,
            lambda i, o: HB.at[at(i, o)],
            lambda i, o, q: HB.at[at(i, o) + (q,)],
            xat[1], xat[3], hs.at[a], hr.at[a],
        )

    tok = gather()
    def step(ring_, t, between=None):
        while True:
            at = next(ring_, t)
            if at == t:
                return
            if between is not None:
                between()

    along_z(1)
    step(tok, 0)

    def cross(a):
        mine = XG.at[a, chip, c]
        there = XS.at[a, 2 * dp + lax.rem(l, 2), c]
        return copy(mine, there, ps.at[a], pr, dev(y, 1 - h, x, 2 * a + lax.rem(l, 2), c))

    def cross_over():
        @pl.when(crossing == 1)
        def _():
            cross(0).start()
            cross(1).start()

    def turn_gain(j, _):
        row = jnp.broadcast_to(gain[pl.ds(j, 1), :], (128, 128))
        GB[j // 3, pl.ds(pl.multiple_of(lax.rem(j, 3) * 128, 128), 128), :] = row.T
        return 0

    load_wi.wait()

    def turn(j, _):
        WT[j] = WI[j].T.reshape(2, 2, 96, HID)
        return 0

    def stats(i):
        def one(o, _):
            j = mod4(y + o) * 4 + mod4(l + i)
            v = XG[0, j].reshape(CHIP, TOK).astype(F32)
            m = jnp.sum(v, axis=0, keepdims=True) * (1.0 / CHIP)
            e = v - m
            SM[pl.ds(4 * i + o, 1), :] = m
            SV[pl.ds(4 * i + o, 1), :] = jnp.sum(e * e, axis=0, keepdims=True)
            return 0

        lax.fori_loop(0, 4, one, 0, unroll=2)

    def share(a, i):
        lp = mod4(l + i)
        b = lax.rem(lp, 2)

        @pl.when(lp // 2 == h)
        def _():
            for o in (1, 3, 2):
                copy(
                    XG.at[a, mod4(x + o) * 4 + lp, c], XS.at[a, 2 * dp + b, c],
                    xs.at[a, b, o], xr.at[a, b, o], xat[o],
                ).start()

    def relay(a):
        for b in range(2):
            for o in (1, 3, 2):
                at = XS.at[a, 2 * (2 * mod4(x + 4 - o) + h) + b, c]
                got(at, xr.at[a, b, o])
                put(at, at, xbs.at[a, b, o], xbr.at[a, b, o], sib)

    def relayed(a):
        own_slice(a).wait()
        for b in range(2):
            for o in (1, 3, 2):
                got(XS.at[a, 2 * (2 * mod4(x + 4 - o) + h) + b, 1 - c], xbr.at[a, b, o])

    def own_slice(a):
        return pltpu.make_async_copy(
            XG.at[a, pl.ds(x * 4 + 2 * h, 2)], XS.at[a, pl.ds(2 * dp, 2)], loc.at[19 + a]
        )

    def gain_step(j, _):
        g = GB[j]
        high = g.astype(BF16)
        low = (g - high.astype(F32)).astype(BF16)
        w = WT[j].reshape(HID, CHIP)
        WG[...] += dot(w, high) + dot(w, low)
        return 0

    def act_step(i):
        def one(o, _):
            j = mod4(y + o) * 4 + mod4(l + i)
            ACT[...] += dot(WO[j], XG[1, j].reshape(CHIP, TOK))
            return 0

        lax.fori_loop(0, 4, one, 0, unroll=True)

    WG[...] = jnp.zeros_like(WG)
    ACT[...] = jnp.zeros_like(ACT)
    lax.fori_loop(0, 8, turn, 0, unroll=2)
    lax.fori_loop(0, 12, turn_gain, 0, unroll=4)
    step(tok, 1)
    lax.fori_loop(8, 16, turn, 0, unroll=2)
    lax.fori_loop(12, 24, turn_gain, 0, unroll=4)
    pass_on(0)
    step(tok, 2)
    share(0, 0)
    lax.fori_loop(24, 48, turn_gain, 0, unroll=4)
    pass_on(1)
    step(tok, 3)
    share(0, 1)
    stats(0)
    for j in range(16):
        load_wo(j).wait()
    lax.fori_loop(0, 8, gain_step, 0, unroll=2)
    pass_on(2)
    step(tok, 4)
    share(0, 2)
    stats(1)
    lax.fori_loop(8, 16, gain_step, 0, unroll=2)
    pass_on(3)
    step(tok, 5)
    share(0, 3)
    stats(2)
    cross_over()
    step(tok, 6)
    share(1, 0)
    stats(3)

    own_slice(0).start()
    means = SM[...]
    mean = jnp.sum(means, axis=0, keepdims=True) * (1.0 / 16)
    off = means - mean
    spread = jnp.sum(SV[...], axis=0, keepdims=True) + CHIP * jnp.sum(off * off, axis=0, keepdims=True)
    inv = lax.rsqrt(spread * (1.0 / D) + 1e-06)
    ST[dp] = jnp.where(lax.broadcasted_iota(jnp.int32, (8, TOK), 0) == 0, mean, inv)
    for o in range(1, 8):
        put(ST.at[dp], ST.at[dp], sts.at[o], str_.at[o], dpat[o])

    def normalise(v, m, r, j):
        return ((v.astype(F32) - m) * r * wide(GB[j])).astype(BF16)

    PRE[...] = jnp.zeros_like(PRE)

    def pre_step(j, _):
        normed = normalise(XG[0, j].reshape(CHIP, TOK), ST[dp, 0:1, :], ST[dp, 1:2, :], j)
        PRE[...] += dot(WT[j].reshape(HID, CHIP), normed)
        return 0

    pieces = [lambda b=b: lax.fori_loop(4 * b, 4 * b + 4, pre_step, 0, unroll=True) for b in range(4)]

    def piece():
        if pieces:
            pieces.pop(0)()

    piece()
    step(tok, 7, piece)
    while pieces:
        piece()

    pre = PRE[...]
    tanh = jnp.tanh(COEF * (pre + 0.044715 * pre * pre * pre))
    HB[0, dp] = (0.5 * pre * (1.0 + tanh)).astype(BF16).reshape(2, 192, TOK)
    SL[...] = 0.5 * (1.0 + tanh) + 0.5 * pre * (1.0 - tanh * tanh) * COEF * (1.0 + 3.0 * 0.044715 * pre * pre)

    def over(a):
        put(HB.at[a, dp], HB.at[a, dp], z4s.at[a], z4r.at[a], opposite)

    over(0)
    ha, hg, sl = hidden_ring(0), hidden_ring(1), slices()
    step(ha, 0)
    share(1, 1)
    act_step(0)
    step(tok, 8)
    share(1, 2)
    act_step(1)
    got(XS.at[slice_at(0, 0, c)], pr)
    slice_along_z((1, 2, 3))
    step(tok, 9)
    share(1, 3)
    step(sl, 0)
    act_step(2)
    step(tok, 10)
    act_step(3)

    HB[1, dp] = (ACT[...] * SL[...]).astype(BF16).reshape(2, 192, TOK)
    over(1)
    step(hg, 0)
    own_slice(1).start()

    own_gain = wide(GB[chip, pl.ds(pl.multiple_of(c * ROWS, ROWS), ROWS), :])

    def own_xhat():
        return (XG[0, chip, c].reshape(ROWS, TOK).astype(F32) - ST[dp, 0:1, :]) * ST[dp, 1:2, :]

    def row_sums():
        grad = HB[1, dp].reshape(HID, TOK).astype(F32)
        side = attn[...].reshape(ROWS, TOK).astype(F32) * own_gain
        s1 = jnp.sum(grad * wide(WG[...]), axis=0, keepdims=True) + jnp.sum(side, axis=0, keepdims=True)
        s2 = jnp.sum(grad * PRE[...], axis=0, keepdims=True) + jnp.sum(side * own_xhat(), axis=0, keepdims=True)
        MO[0] = jnp.where(lax.broadcasted_iota(jnp.int32, (8, TOK), 0) == 0, s1, s2)
        put(MO.at[0], MO.at[1], mos.at[0], mor.at[0], sib)

    def row_sums_y():
        got(MO.at[1], mor.at[0])
        MO[2] = MO[0] + MO[1]
        for o in (1, 2, 3):
            put(MO.at[2], MO.at[2 + o], mos.at[o], mor.at[o], yat[o])

    def row_sums_z():
        for o in (1, 2, 3):
            got(MO.at[2 + o], mor.at[o])
        MO[6] = MO[2] + MO[3] + MO[4] + MO[5]
        for o in (1, 2, 3):
            put(MO.at[6], MO.at[6 + o], mos.at[3 + o], mor.at[3 + o], zat[o])

    def partial(o):
        def one(n, _):
            q = mod4(l + 1 + n)
            j = mod4(y + o) * 4 + q
            part = dot(WI[j], HB[1, dp].reshape(HID, TOK))
            WT[j] = part.astype(BF16).reshape(2, 2, 96, TOK)
            copy(WT.at[j, 1 - c], R1.at[j], r1s.at[o, q], r1r.at[o, q], sib).start()
            return 0

        lax.fori_loop(0, 4, one, 0, unroll=True)

    def both(j, o, q):
        got(R1.at[j], r1r.at[o, q])
        return WT[j, c].astype(F32) + R1[j].astype(F32)

    partial(2)
    next(ha)
    partial(1)

    def far(n, _):
        q = mod4(l + 1 + n)
        j = mod4(y + 2) * 4 + q
        WT[j, c] = both(j, 2, q).astype(BF16)
        copy(WT.at[j, c, 0], R2.at[0, q], r2s.at[0, q], r2r.at[0, q], yat[1]).start()
        copy(WT.at[j, c, 1], R2.at[1, q], r2s.at[1, q], r2r.at[1, q], yat[3]).start()
        return 0

    lax.fori_loop(0, 4, far, 0)
    partial(3)
    row_sums()
    partial(0)
    step(ha, 1)
    step(sl, 1)
    row_sums_y()

    def near(n, _):
        q = mod4(l + 1 + n)
        for o, w in ((1, 0), (3, 1)):
            j = mod4(y + o) * 4 + q
            total = both(j, o, q)
            got(R2.at[w, q], r2r.at[w, q])
            WT[j, c, w] = (total[w] + R2[w, q].astype(F32)).astype(BF16)
            WT[j, c, 1 - w] = total[1 - w].astype(BF16)
            copy(WT.at[j, c], R3.at[w, q], r3s.at[w, q], r3r.at[w, q], yat[o]).start()
        return 0

    lax.fori_loop(0, 2, near, 0)
    next(hg)
    lax.fori_loop(2, 4, near, 0)

    def norm_of(hh):
        def one(o, _):
            d = 2 * mod4(x + o) + hh
            for b in range(2):
                XN[2 * d + b] = normalise(
                    XS[0, 2 * d + b].reshape(CHIP, TOK), ST[d, 0:1, :], ST[d, 1:2, :], 2 * dp + b
                )
            return 0

        lax.fori_loop(0, 4, one, 0, unroll=2)

    def sum_in(hh):
        def one(o, _):
            d = 2 * mod4(x + o) + hh
            dwin_out[...] += dot_nt(XN[pl.ds(2 * d, 2)].reshape(768, TOK), HB[1, d].reshape(HID, TOK))
            return 0

        lax.fori_loop(0, 4, one, 0, unroll=2)

    def sum_out(hh):
        def one(o, _):
            d = 2 * mod4(x + o) + hh
            dwout_out[...] += dot_nt(HB[0, d].reshape(HID, TOK), XS[1, pl.ds(2 * d, 2)].reshape(768, TOK))
            return 0

        lax.fori_loop(0, 4, one, 0, unroll=2)

    dwin_out[...] = jnp.zeros_like(dwin_out)
    dwout_out[...] = jnp.zeros_like(dwout_out)
    row_sums_z()
    step(ha, 2)
    relay(0)
    relay(1)
    step(sl, 2)
    for o in range(1, 8):
        got(ST.at[lax.rem(dp + 8 - o, 8)], str_.at[o])
    relayed(0)
    norm_of(h)
    step(hg, 1)
    relayed(1)
    sum_out(h)

    def collect(k):
        q = mod4(l + k)
        j = y * 4 + q
        got(R3.at[0, q], r3r.at[0, q])
        got(R3.at[1, q], r3r.at[1, q])
        return both(j, 0, q) + R3[0, q].astype(F32) + R3[1, q].astype(F32)

    for k in (1, 2, 3):
        j = y * 4 + mod4(l + k)
        WT[j, c] = collect(k).astype(BF16)
        put(WT.at[j, c], R4.at[k], r4s.at[k], r4r.at[k], zat[k])
    TS[...] = collect(0)
    step(sl, 3)
    step(hg, 2)
    for k in (1, 2, 3):
        got(R4.at[k], r4r.at[k])

    ng = TS[...] + R4[1].astype(F32) + R4[2].astype(F32) + R4[3].astype(F32) + attn[...].astype(F32)
    ng = ng.reshape(ROWS, TOK)
    xhat = own_xhat()
    prod = ng * xhat
    prod = prod[:, 0:128] + prod[:, 128:256] + prod[:, 256:384]
    prod = jnp.concatenate([prod, jnp.zeros((64, 128), F32)], axis=0).T
    GP[dp] = jnp.broadcast_to(jnp.sum(prod, axis=0, keepdims=True), (8, 256))
    for o in range(1, 8):
        put(GP.at[dp], GP.at[dp], gps.at[o], gpr.at[o], dpat[o])
    step(sl, 4)
    for o in (1, 2, 3):
        got(MO.at[6 + o], mor.at[3 + o])
    sums = (MO[6] + MO[7] + MO[8] + MO[9]) * (1.0 / D)
    dx_out[...] = (
        XG[1, chip, c].reshape(ROWS, TOK).astype(F32)
        + (ng * own_gain - sums[0:1, :] - xhat * sums[1:2, :]) * ST[dp, 1:2, :]
    ).astype(BF16)
    sum_in(h)
    step(sl, 5)
    step(sl, 6)
    step(ha, 4)
    for o in range(1, 8):
        got(GP.at[lax.rem(dp + 8 - o, 8)], gpr.at[o])
    total = GP[0]
    for o in range(1, 8):
        total = total + GP[o]
    gg_out[...] = total[0:1, 0:ROWS]
    norm_of(1 - h)
    sum_out(1 - h)
    step(hg, 4)
    sum_in(1 - h)

    for made in sends:
        made.wait_send()
    for a in range(2):
        for b in range(2):
            for o in (1, 2, 3):
                copy(
                    XG.at[a, mod4(x + o) * 4 + 2 * h + b, c], XS.at[a, 2 * dp + b, c],
                    xs.at[a, b, o], xr.at[a, b, o], xat[o],
                ).wait_send()

    @pl.when(crossing == 1)
    def _():
        cross(0).wait_send()
        cross(1).wait_send()

    def left(q, _):
        for o in range(4):
            j = mod4(y + o) * 4 + q
            copy(WT.at[j, 1 - c], R1.at[j], r1s.at[o, q], r1r.at[o, q], sib).wait_send()
        j = mod4(y + 2) * 4 + q
        copy(WT.at[j, c, 0], R2.at[0, q], r2s.at[0, q], r2r.at[0, q], yat[1]).wait_send()
        copy(WT.at[j, c, 1], R2.at[1, q], r2s.at[1, q], r2r.at[1, q], yat[3]).wait_send()
        for o, w in ((1, 0), (3, 1)):
            j = mod4(y + o) * 4 + q
            copy(WT.at[j, c], R3.at[w, q], r3s.at[w, q], r3r.at[w, q], yat[o]).wait_send()
        return 0

    lax.fori_loop(0, 4, left, 0)


def hand_over(*refs):
    sources, results, between, sems = refs[:4], refs[4:8], refs[8:12], refs[12]
    arrive = [pltpu.make_async_copy(a, b, sems.at[0, i]) for i, (a, b) in enumerate(zip(sources, between))]
    leave = [pltpu.make_async_copy(a, b, sems.at[1, i]) for i, (a, b) in enumerate(zip(between, results))]
    for made in arrive:
        made.start()
    for one, two in zip(arrive, leave):
        one.wait()
        two.start()
    for made in leave:
        made.wait()


def on_device(block_input, output_gradient, attn_grad, layernorm_gain, w_in, w_out):
    vmem, anywhere = pl.BlockSpec(memory_space=pltpu.VMEM), pl.BlockSpec(memory_space=pl.ANY)
    dma = pltpu.SemaphoreType.DMA
    pair = lambda *shape: [dma(shape), dma(shape)]
    scratch = [
        pltpu.VMEM((2, 16, 2, 2, 96, TOK), BF16),
        pltpu.VMEM((2, 16, 2, 2, 96, TOK), BF16),
        pltpu.VMEM((16, CHIP, TOK), BF16),
        pltpu.VMEM((16, CHIP, HID), BF16),
        pltpu.VMEM((16, 2, 2, 96, TOK), BF16),
        pltpu.VMEM((16, HID, CHIP), BF16),
        pltpu.VMEM((2, 8, 2, 192, TOK), BF16),
        pltpu.VMEM((16, CHIP, 128), F32),
        pltpu.VMEM((HID, TOK), F32),
        pltpu.VMEM((HID, TOK), F32),
        pltpu.VMEM((HID, TOK), F32),
        pltpu.VMEM((HID, 128), F32),
        pltpu.VMEM((16, TOK), F32),
        pltpu.VMEM((16, TOK), F32),
        pltpu.VMEM((8, 8, TOK), F32),
        pltpu.VMEM((16, 2, 96, TOK), BF16),
        pltpu.VMEM((2, 4, 96, TOK), BF16),
        pltpu.VMEM((2, 4, 2, 96, TOK), BF16),
        pltpu.VMEM((4, 2, 96, TOK), BF16),
        pltpu.VMEM((2, 96, TOK), F32),
        pltpu.VMEM((10, 8, TOK), F32),
        pltpu.VMEM((8, 8, 256), F32),
    ]
    scratch += pair(2, 4) + pair(8, 8) + pair(4) + pair(4, 8) + [dma((2,)), dma]
    scratch += pair(2, 2, 4) + pair(2) + pair(2, 2, 4) + pair(2, 2, 4)
    scratch += [pltpu.SemaphoreType.REGULAR] * 4
    scratch += pair(4, 4) + pair(2, 4) + pair(2, 4) + pair(4) + pair(8) + pair(7) + pair(8) + [dma((21,))]
    shapes = (
        jax.ShapeDtypeStruct((ROWS, TOK), BF16),
        jax.ShapeDtypeStruct((1, ROWS), F32),
        jax.ShapeDtypeStruct((768, HID), F32),
        jax.ShapeDtypeStruct((HID, 768), F32),
    )
    results = pl.pallas_call(
        kernel,
        out_shape=shapes,
        in_specs=[anywhere, anywhere, vmem, vmem, anywhere, anywhere],
        out_specs=(vmem,) * 4,
        scratch_shapes=scratch,
        compiler_params=pltpu.CompilerParams(
            collective_id=0, has_side_effects=True, vmem_limit_bytes=62 * 2**20
        ),
        cost_estimate=pl.CostEstimate(flops=9 * 10**9, bytes_accessed=12 * 10**6, transcendentals=147456),
        name="parallel_block_backward",
    )(
        block_input.T.reshape(2, 96, TOK),
        output_gradient.T.reshape(2, 96, TOK),
        attn_grad.T.reshape(2, 96, TOK),
        layernorm_gain.reshape(48, 128),
        w_in.reshape(16, CHIP, HID),
        w_out,
    )
    dx, dgain, dw_in, dw_out = pl.pallas_call(
        hand_over,
        out_shape=shapes,
        in_specs=[anywhere] * 4,
        out_specs=(anywhere,) * 4,
        scratch_shapes=[pltpu.VMEM(s.shape, s.dtype) for s in shapes] + [dma((2, 4))],
        name="results",
    )(*results)
    return dx.T, dgain.reshape(ROWS), dw_in, dw_out


def solution(mesh):
    token = P("dp", "tensor")
    return jax.shard_map(
        on_device,
        mesh=mesh,
        in_specs=(token, token, token, P(), P(None, "tensor"), P("tensor", None)),
        out_specs=(token, P("tensor"), P("dp", "tensor"), P("tensor", "dp")),
        check_vma=False,
    )
```

```python
import functools
import math

import jax
import jax.numpy as jnp
from jax import lax
from jax.experimental import pallas as pl
from jax.experimental.pallas import tpu as pltpu
from jax.sharding import PartitionSpec as P

MESH = pl.DeviceIdType.MESH
F32, BF16 = jnp.float32, jnp.bfloat16
COEF = math.sqrt(2.0 / math.pi)
TOK = 384
HID = 384
ROWS = 192
CHIP = 384
D = 6144

NT = (((1,), (1,)), ((), ()))


def dot(a, b):
    return jnp.dot(a, b, preferred_element_type=F32)


def dot_nt(a, b):
    return lax.dot_general(a, b, NT, preferred_element_type=F32)


def wide(column):
    return jnp.concatenate([column] * (TOK // 128), axis=1)


def kernel(
    x_in, g_in, attn, gain, w_in, w_out,
    dx_out, gg_out, dwin_out, dwout_hbm,
    XG, XS, XN, WI, WT, WO, HB, GB, PRE, ACT, SL, WG, dwout_out, SM, SV, ST, R1, R2, R3, R4, TS, MO, GP,
    zs, zr, as_, ar, z2s, z2r, a2s, a2r, ps, pr, hs, hr, z4s, z4r, xs, xr, xbs, xbr, half_in, line_in, x_in_, y_in_,
    r1s, r1r, r2s, r2r, r3s, r3r, r4s, r4r, sts, str_, mos, mor, gps, gpr, loc,
):
    dp, tensor = lax.axis_index("dp"), lax.axis_index("tensor")
    x, h = dp // 2, dp % 2
    y, l, c = tensor // 8, (tensor // 2) % 4, tensor % 2
    chip = y * 4 + l

    def dev(x_, h_, y_, l_, c_):
        return (x_ * 2 + h_, y_ * 8 + l_ * 2 + c_)

    def mod4(v):
        return lax.rem(v, 4)

    sib = dev(x, h, y, l, 1 - c)
    yat = [dev(x, h, mod4(y + o), l, c) for o in range(4)]
    zat = [dev(x, h, y, mod4(l + o), c) for o in range(4)]
    xat = [dev(mod4(x + o), h, y, l, c) for o in range(4)]
    opposite = dev(x, 1 - h, y, l, c)
    dpat = [(lax.rem(dp + o, 8), tensor) for o in range(8)]
    crossing = lax.rem(l // 2 + h, 2)

    sends = []

    def copy(src, dst, send, recv, to):
        return pltpu.make_async_remote_copy(
            src_ref=src, dst_ref=dst, send_sem=send, recv_sem=recv, device_id=to, device_id_type=MESH
        )

    def put(src, dst, send, recv, to):
        made = copy(src, dst, send, recv, to)
        made.start()
        sends.append(made)

    def got(dst, recv):
        copy(dst, dst, recv, recv, sib).wait_recv()

    barrier = pltpu.get_barrier_semaphore()
    for to in [sib] + yat[1:] + zat[1:] + xat[1:]:
        pl.semaphore_signal(barrier, inc=1, device_id=to, device_id_type=MESH)

    @pl.when(l == 0)
    def _():
        pl.semaphore_signal(barrier, inc=1, device_id=dev(x, 1 - h, y, 3, c), device_id_type=MESH)

    @pl.when(l == 3)
    def _():
        pl.semaphore_signal(barrier, inc=1, device_id=dev(x, 1 - h, y, 0, c), device_id_type=MESH)

    own_x = pltpu.make_async_copy(x_in, XG.at[0, chip, c], loc.at[0])
    own_g = pltpu.make_async_copy(g_in, XG.at[1, chip, c], loc.at[1])
    load_wi = pltpu.make_async_copy(w_in, WI, loc.at[2])
    own_x.start()
    own_g.start()
    load_wi.start()

    def load_wo(j):
        return pltpu.make_async_copy(w_out.at[:, pl.ds(j * CHIP, CHIP)], WO.at[j], loc.at[3 + j])

    for j in range(16):
        load_wo(j).start()
    own_x.wait()
    own_g.wait()
    pl.semaphore_wait(barrier, jnp.where(lax.rem(l, 3) == 0, 11, 10))

    @pl.when(l == 0)
    def _():
        pl.semaphore_signal(half_in, inc=1, device_id=dev(x, 1 - h, y, 3, c), device_id_type=MESH)

    def pass_on(step):
        if step == 0:
            @pl.when(l == 3)
            def _():
                pl.semaphore_wait(half_in, 1)
                for to in zat[1:]:
                    pl.semaphore_signal(line_in, inc=1, device_id=to, device_id_type=MESH)
        if step == 1:
            @pl.when(l < 3)
            def _():
                pl.semaphore_wait(line_in, 1)

            for to in xat[1:]:
                pl.semaphore_signal(x_in_, inc=1, device_id=to, device_id_type=MESH)
        if step == 2:
            pl.semaphore_wait(x_in_, 3)
            for to in yat[1:]:
                pl.semaphore_signal(y_in_, inc=1, device_id=to, device_id_type=MESH)
        if step == 3:
            pl.semaphore_wait(y_in_, 3)

    def ring(n, ready, view, half, plus, minus, ss, rs, other=None):
        def first(i):
            ready(i)
            put(view(i, 0), view(i, 0), ss.at[i, 0], rs.at[i, 1], plus)
            put(view(i, 0), view(i, 0), ss.at[i, 1], rs.at[i, 0], minus)
            if other:
                put(view(i, 0), view(i, 0), ss.at[i, 4], rs.at[i, 4], sib)

        def second(i):
            got(view(i, 1), rs.at[i, 0])
            put(half(i, 1, 1), half(i, 1, 1), ss.at[i, 3], rs.at[i, 3], minus)
            got(view(i, 3), rs.at[i, 1])
            put(half(i, 3, 0), half(i, 3, 0), ss.at[i, 2], rs.at[i, 2], plus)
            if other:
                put(view(i, 1), view(i, 1), ss.at[i, 5], rs.at[i, 5], sib)
                put(view(i, 3), view(i, 3), ss.at[i, 7], rs.at[i, 7], sib)

        def third(i):
            got(half(i, 2, 0), rs.at[i, 2])
            got(half(i, 2, 1), rs.at[i, 3])
            if other:
                put(view(i, 2), view(i, 2), ss.at[i, 6], rs.at[i, 6], sib)

        def last(i):
            if other:
                for o in (0, 1, 3, 2):
                    got(other(i, o), rs.at[i, 4 + o])

        for t in range(n + 3):
            if t < n and other:
                first(t)
                yield None
            if 0 <= t - 1 < n:
                second(t - 1)
                yield None
            if t < n and not other:
                first(t)
                yield None
            if 0 <= t - 2 < n:
                third(t - 2)
                yield None
            if 0 <= t - 3 < n:
                last(t - 3)
            yield t

    def chip_at(i, o):
        return mod4(y + o) * 4 + mod4(l + i)

    queue = [(a, k) for a in range(2) for k in (1, 2, 3)]

    def along_z(count):
        for a, k in queue[:count]:
            put(XG.at[a, chip, c], XG.at[a, chip, c], zs.at[a, k], zr.at[a, k], zat[4 - k])
        del queue[:count]

    order = [(a, k) for a in range(2) for k in range(4)]

    def gather():
        def block(i, o, c_):
            a, k = order[i]
            return XG.at[a, chip_at(k, o), c_]

        def ready(i):
            a, k = order[i]
            if k > 0:
                got(block(i, 0, c), zr.at[a, k])
            if i > 0:
                along_z(1)

        return ring(
            8, ready,
            lambda i, o: block(i, o, c),
            lambda i, o, q: XG.at[order[i][0], chip_at(order[i][1], o), c, q],
            yat[1], yat[3], as_, ar,
            lambda i, o: block(i, o, 1 - c),
        )

    def slice_at(i, o, c_):
        lp = mod4(l + i)
        return (lp // 2, 2 * (2 * mod4(y + o) + (1 - h)) + lax.rem(lp, 2), c_)

    def slice_along_z(ks):
        for k in ks:
            put(XS.at[slice_at(0, 0, c)], XS.at[slice_at(0, 0, c)], z2s.at[k], z2r.at[k], zat[4 - k])

    def slices():
        def ready(i):
            if i > 0:
                got(XS.at[slice_at(i, 0, c)], z2r.at[i])

        return ring(
            4, ready,
            lambda i, o: XS.at[slice_at(i, o, c)],
            lambda i, o, q: XS.at[slice_at(i, o, c) + (q,)],
            yat[1], yat[3], a2s, a2r,
            lambda i, o: XS.at[slice_at(i, o, 1 - c)],
        )

    def hidden_ring(a):
        def at(i, o):
            return (a, 2 * mod4(x + o) + (h if i == 0 else 1 - h))

        def ready(i):
            if i > 0:
                got(HB.at[at(1, 0)], z4r.at[a])

        return ring(
            2, ready,
            lambda i, o: HB.at[at(i, o)],
            lambda i, o, q: HB.at[at(i, o) + (q,)],
            xat[1], xat[3], hs.at[a], hr.at[a],
        )

    tok = gather()
    def step(ring_, t, between=None):
        while True:
            at = next(ring_, t)
            if at == t:
                return
            if between is not None:
                between()

    along_z(1)
    step(tok, 0)

    def cross(a):
        mine = XG.at[a, chip, c]
        there = XS.at[a, 2 * dp + lax.rem(l, 2), c]
        return copy(mine, there, ps.at[a], pr, dev(y, 1 - h, x, 2 * a + lax.rem(l, 2), c))

    def cross_over():
        @pl.when(crossing == 1)
        def _():
            cross(0).start()
            cross(1).start()

    def turn_gain(j, _):
        row = jnp.broadcast_to(gain[pl.ds(j, 1), :], (128, 128))
        GB[j // 3, pl.ds(pl.multiple_of(lax.rem(j, 3) * 128, 128), 128), :] = row.T
        return 0

    load_wi.wait()

    def turn(j, _):
        WT[j] = WI[j].T.reshape(2, 2, 96, HID)
        return 0

    def stats(i):
        def one(o, _):
            j = mod4(y + o) * 4 + mod4(l + i)
            v = XG[0, j].reshape(CHIP, TOK).astype(F32)
            m = jnp.sum(v, axis=0, keepdims=True) * (1.0 / CHIP)
            e = v - m
            SM[pl.ds(4 * i + o, 1), :] = m
            SV[pl.ds(4 * i + o, 1), :] = jnp.sum(e * e, axis=0, keepdims=True)
            return 0

        lax.fori_loop(0, 4, one, 0, unroll=2)

    def share(a, i):
        lp = mod4(l + i)
        b = lax.rem(lp, 2)

        @pl.when(lp // 2 == h)
        def _():
            for o in (1, 3, 2):
                copy(
                    XG.at[a, mod4(x + o) * 4 + lp, c], XS.at[a, 2 * dp + b, c],
                    xs.at[a, b, o], xr.at[a, b, o], xat[o],
                ).start()

    def relay(a):
        for b in range(2):
            for o in (1, 3, 2):
                at = XS.at[a, 2 * (2 * mod4(x + 4 - o) + h) + b, c]
                got(at, xr.at[a, b, o])
                put(at, at, xbs.at[a, b, o], xbr.at[a, b, o], sib)

    def relayed(a):
        own_slice(a).wait()
        for b in range(2):
            for o in (1, 3, 2):
                got(XS.at[a, 2 * (2 * mod4(x + 4 - o) + h) + b, 1 - c], xbr.at[a, b, o])

    def own_slice(a):
        return pltpu.make_async_copy(
            XG.at[a, pl.ds(x * 4 + 2 * h, 2)], XS.at[a, pl.ds(2 * dp, 2)], loc.at[19 + a]
        )

    def gain_step(j, _):
        g = GB[j]
        high = g.astype(BF16)
        low = (g - high.astype(F32)).astype(BF16)
        w = WT[j].reshape(HID, CHIP)
        WG[...] += dot(w, high) + dot(w, low)
        return 0

    def act_step(i):
        def one(o, _):
            j = mod4(y + o) * 4 + mod4(l + i)
            ACT[...] += dot(WO[j], XG[1, j].reshape(CHIP, TOK))
            return 0

        lax.fori_loop(0, 4, one, 0, unroll=True)

    WG[...] = jnp.zeros_like(WG)
    ACT[...] = jnp.zeros_like(ACT)
    lax.fori_loop(0, 8, turn, 0, unroll=2)
    lax.fori_loop(0, 12, turn_gain, 0, unroll=4)
    step(tok, 1)
    lax.fori_loop(8, 16, turn, 0, unroll=2)
    lax.fori_loop(12, 24, turn_gain, 0, unroll=4)
    pass_on(0)
    step(tok, 2)
    share(0, 0)
    lax.fori_loop(24, 48, turn_gain, 0, unroll=4)
    pass_on(1)
    step(tok, 3)
    share(0, 1)
    stats(0)
    for j in range(16):
        load_wo(j).wait()
    lax.fori_loop(0, 8, gain_step, 0, unroll=2)
    pass_on(2)
    step(tok, 4)
    share(0, 2)
    stats(1)
    lax.fori_loop(8, 16, gain_step, 0, unroll=2)
    pass_on(3)
    step(tok, 5)
    share(0, 3)
    stats(2)
    cross_over()
    step(tok, 6)
    share(1, 0)
    stats(3)

    own_slice(0).start()
    means = SM[...]
    mean = jnp.sum(means, axis=0, keepdims=True) * (1.0 / 16)
    off = means - mean
    spread = jnp.sum(SV[...], axis=0, keepdims=True) + CHIP * jnp.sum(off * off, axis=0, keepdims=True)
    inv = lax.rsqrt(spread * (1.0 / D) + 1e-06)
    ST[dp] = jnp.where(lax.broadcasted_iota(jnp.int32, (8, TOK), 0) == 0, mean, inv)
    for o in range(1, 8):
        put(ST.at[dp], ST.at[dp], sts.at[o], str_.at[o], dpat[o])

    def normalise(v, m, r, j):
        return ((v.astype(F32) - m) * r * wide(GB[j])).astype(BF16)

    PRE[...] = jnp.zeros_like(PRE)

    def pre_step(j, _):
        normed = normalise(XG[0, j].reshape(CHIP, TOK), ST[dp, 0:1, :], ST[dp, 1:2, :], j)
        PRE[...] += dot(WT[j].reshape(HID, CHIP), normed)
        return 0

    pieces = [lambda b=b: lax.fori_loop(4 * b, 4 * b + 4, pre_step, 0, unroll=True) for b in range(4)]

    def piece():
        if pieces:
            pieces.pop(0)()

    piece()
    step(tok, 7, piece)
    while pieces:
        piece()

    pre = PRE[...]
    tanh = jnp.tanh(COEF * (pre + 0.044715 * pre * pre * pre))
    HB[0, dp] = (0.5 * pre * (1.0 + tanh)).astype(BF16).reshape(2, 192, TOK)
    SL[...] = 0.5 * (1.0 + tanh) + 0.5 * pre * (1.0 - tanh * tanh) * COEF * (1.0 + 3.0 * 0.044715 * pre * pre)

    def over(a):
        put(HB.at[a, dp], HB.at[a, dp], z4s.at[a], z4r.at[a], opposite)

    over(0)
    ha, hg, sl = hidden_ring(0), hidden_ring(1), slices()
    step(ha, 0)
    share(1, 1)
    act_step(0)
    step(tok, 8)
    share(1, 2)
    act_step(1)
    got(XS.at[slice_at(0, 0, c)], pr)
    slice_along_z((1, 2, 3))
    step(tok, 9)
    share(1, 3)
    step(sl, 0)
    act_step(2)
    step(tok, 10)
    act_step(3)

    HB[1, dp] = (ACT[...] * SL[...]).astype(BF16).reshape(2, 192, TOK)
    over(1)
    step(hg, 0)
    own_slice(1).start()

    own_gain = wide(GB[chip, pl.ds(pl.multiple_of(c * ROWS, ROWS), ROWS), :])

    def own_xhat():
        return (XG[0, chip, c].reshape(ROWS, TOK).astype(F32) - ST[dp, 0:1, :]) * ST[dp, 1:2, :]

    def row_sums():
        grad = HB[1, dp].reshape(HID, TOK).astype(F32)
        side = attn[...].reshape(ROWS, TOK).astype(F32) * own_gain
        s1 = jnp.sum(grad * wide(WG[...]), axis=0, keepdims=True) + jnp.sum(side, axis=0, keepdims=True)
        s2 = jnp.sum(grad * PRE[...], axis=0, keepdims=True) + jnp.sum(side * own_xhat(), axis=0, keepdims=True)
        MO[0] = jnp.where(lax.broadcasted_iota(jnp.int32, (8, TOK), 0) == 0, s1, s2)
        put(MO.at[0], MO.at[1], mos.at[0], mor.at[0], sib)

    def row_sums_y():
        got(MO.at[1], mor.at[0])
        MO[2] = MO[0] + MO[1]
        for o in (1, 2, 3):
            put(MO.at[2], MO.at[2 + o], mos.at[o], mor.at[o], yat[o])

    def row_sums_z():
        for o in (1, 2, 3):
            got(MO.at[2 + o], mor.at[o])
        MO[6] = MO[2] + MO[3] + MO[4] + MO[5]
        for o in (1, 2, 3):
            put(MO.at[6], MO.at[6 + o], mos.at[3 + o], mor.at[3 + o], zat[o])

    def partial(o):
        def one(n, _):
            q = mod4(l + 1 + n)
            j = mod4(y + o) * 4 + q
            part = dot(WI[j], HB[1, dp].reshape(HID, TOK))
            WT[j] = part.astype(BF16).reshape(2, 2, 96, TOK)
            copy(WT.at[j, 1 - c], R1.at[j], r1s.at[o, q], r1r.at[o, q], sib).start()
            return 0

        lax.fori_loop(0, 4, one, 0, unroll=True)

    def both(j, o, q):
        got(R1.at[j], r1r.at[o, q])
        return WT[j, c].astype(F32) + R1[j].astype(F32)

    partial(2)
    next(ha)
    partial(1)

    def far(n, _):
        q = mod4(l + 1 + n)
        j = mod4(y + 2) * 4 + q
        WT[j, c] = both(j, 2, q).astype(BF16)
        copy(WT.at[j, c, 0], R2.at[0, q], r2s.at[0, q], r2r.at[0, q], yat[1]).start()
        copy(WT.at[j, c, 1], R2.at[1, q], r2s.at[1, q], r2r.at[1, q], yat[3]).start()
        return 0

    lax.fori_loop(0, 4, far, 0)
    partial(3)
    row_sums()
    partial(0)
    step(ha, 1)
    step(sl, 1)
    row_sums_y()

    def near(n, _):
        q = mod4(l + 1 + n)
        for o, w in ((1, 0), (3, 1)):
            j = mod4(y + o) * 4 + q
            total = both(j, o, q)
            got(R2.at[w, q], r2r.at[w, q])
            WT[j, c, w] = (total[w] + R2[w, q].astype(F32)).astype(BF16)
            WT[j, c, 1 - w] = total[1 - w].astype(BF16)
            copy(WT.at[j, c], R3.at[w, q], r3s.at[w, q], r3r.at[w, q], yat[o]).start()
        return 0

    lax.fori_loop(0, 2, near, 0)
    next(hg)
    lax.fori_loop(2, 4, near, 0)

    def norm_of(hh):
        def one(o, _):
            d = 2 * mod4(x + o) + hh
            for b in range(2):
                XN[2 * d + b] = normalise(
                    XS[0, 2 * d + b].reshape(CHIP, TOK), ST[d, 0:1, :], ST[d, 1:2, :], 2 * dp + b
                )
            return 0

        lax.fori_loop(0, 4, one, 0, unroll=2)

    def sum_in(hh):
        def one(o, _):
            d = 2 * mod4(x + o) + hh
            dwin_out[...] += dot_nt(XN[pl.ds(2 * d, 2)].reshape(768, TOK), HB[1, d].reshape(HID, TOK))
            return 0

        lax.fori_loop(0, 4, one, 0, unroll=2)

    def sum_out(hh):
        def one(o, _):
            d = 2 * mod4(x + o) + hh
            dwout_out[...] += dot_nt(HB[0, d].reshape(HID, TOK), XS[1, pl.ds(2 * d, 2)].reshape(768, TOK))
            return 0

        lax.fori_loop(0, 4, one, 0, unroll=2)

    dwin_out[...] = jnp.zeros_like(dwin_out)
    dwout_out[...] = jnp.zeros_like(dwout_out)
    row_sums_z()
    step(ha, 2)
    relay(0)
    relay(1)
    step(sl, 2)
    for o in range(1, 8):
        got(ST.at[lax.rem(dp + 8 - o, 8)], str_.at[o])
    relayed(0)
    norm_of(h)
    step(hg, 1)
    relayed(1)
    sum_out(h)

    def collect(k):
        q = mod4(l + k)
        j = y * 4 + q
        got(R3.at[0, q], r3r.at[0, q])
        got(R3.at[1, q], r3r.at[1, q])
        return both(j, 0, q) + R3[0, q].astype(F32) + R3[1, q].astype(F32)

    for k in (1, 2, 3):
        j = y * 4 + mod4(l + k)
        WT[j, c] = collect(k).astype(BF16)
        put(WT.at[j, c], R4.at[k], r4s.at[k], r4r.at[k], zat[k])
    TS[...] = collect(0)
    step(sl, 3)
    step(hg, 2)
    for k in (1, 2, 3):
        got(R4.at[k], r4r.at[k])

    ng = TS[...] + R4[1].astype(F32) + R4[2].astype(F32) + R4[3].astype(F32) + attn[...].astype(F32)
    ng = ng.reshape(ROWS, TOK)
    xhat = own_xhat()
    prod = ng * xhat
    prod = prod[:, 0:128] + prod[:, 128:256] + prod[:, 256:384]
    prod = jnp.concatenate([prod, jnp.zeros((64, 128), F32)], axis=0).T
    GP[dp] = jnp.broadcast_to(jnp.sum(prod, axis=0, keepdims=True), (8, 256))
    for o in range(1, 8):
        put(GP.at[dp], GP.at[dp], gps.at[o], gpr.at[o], dpat[o])
    step(sl, 4)
    for o in (1, 2, 3):
        got(MO.at[6 + o], mor.at[3 + o])
    sums = (MO[6] + MO[7] + MO[8] + MO[9]) * (1.0 / D)
    dx_out[...] = (
        XG[1, chip, c].reshape(ROWS, TOK).astype(F32)
        + (ng * own_gain - sums[0:1, :] - xhat * sums[1:2, :]) * ST[dp, 1:2, :]
    ).astype(BF16)
    sum_in(h)
    step(sl, 5)
    step(sl, 6)
    step(ha, 4)
    for o in range(1, 8):
        got(GP.at[lax.rem(dp + 8 - o, 8)], gpr.at[o])
    total = GP[0]
    for o in range(1, 8):
        total = total + GP[o]
    gg_out[...] = total[0:1, 0:ROWS]
    norm_of(1 - h)
    sum_out(1 - h)
    leave = pltpu.make_async_copy(dwout_out, dwout_hbm, loc.at[21])
    leave.start()
    step(hg, 4)
    sum_in(1 - h)
    leave.wait()

    for made in sends:
        made.wait_send()
    for a in range(2):
        for b in range(2):
            for o in (1, 2, 3):
                copy(
                    XG.at[a, mod4(x + o) * 4 + 2 * h + b, c], XS.at[a, 2 * dp + b, c],
                    xs.at[a, b, o], xr.at[a, b, o], xat[o],
                ).wait_send()

    @pl.when(crossing == 1)
    def _():
        cross(0).wait_send()
        cross(1).wait_send()

    def left(q, _):
        for o in range(4):
            j = mod4(y + o) * 4 + q
            copy(WT.at[j, 1 - c], R1.at[j], r1s.at[o, q], r1r.at[o, q], sib).wait_send()
        j = mod4(y + 2) * 4 + q
        copy(WT.at[j, c, 0], R2.at[0, q], r2s.at[0, q], r2r.at[0, q], yat[1]).wait_send()
        copy(WT.at[j, c, 1], R2.at[1, q], r2s.at[1, q], r2r.at[1, q], yat[3]).wait_send()
        for o, w in ((1, 0), (3, 1)):
            j = mod4(y + o) * 4 + q
            copy(WT.at[j, c], R3.at[w, q], r3s.at[w, q], r3r.at[w, q], yat[o]).wait_send()
        return 0

    lax.fori_loop(0, 4, left, 0)


def hand_over(*refs):
    sources, results, between, sems = refs[:4], refs[4:8], refs[8:12], refs[12]
    arrive = [pltpu.make_async_copy(a, b, sems.at[0, i]) for i, (a, b) in enumerate(zip(sources, between))]
    leave = [pltpu.make_async_copy(a, b, sems.at[1, i]) for i, (a, b) in enumerate(zip(between, results))]
    for made in arrive:
        made.start()
    for one, two in zip(arrive, leave):
        one.wait()
        two.start()
    for made in leave:
        made.wait()


def on_device(block_input, output_gradient, attn_grad, layernorm_gain, w_in, w_out):
    vmem, anywhere = pl.BlockSpec(memory_space=pltpu.VMEM), pl.BlockSpec(memory_space=pl.ANY)
    dma = pltpu.SemaphoreType.DMA
    pair = lambda *shape: [dma(shape), dma(shape)]
    scratch = [
        pltpu.VMEM((2, 16, 2, 2, 96, TOK), BF16),
        pltpu.VMEM((2, 16, 2, 2, 96, TOK), BF16),
        pltpu.VMEM((16, CHIP, TOK), BF16),
        pltpu.VMEM((16, CHIP, HID), BF16),
        pltpu.VMEM((16, 2, 2, 96, TOK), BF16),
        pltpu.VMEM((16, HID, CHIP), BF16),
        pltpu.VMEM((2, 8, 2, 192, TOK), BF16),
        pltpu.VMEM((16, CHIP, 128), F32),
        pltpu.VMEM((HID, TOK), F32),
        pltpu.VMEM((HID, TOK), F32),
        pltpu.VMEM((HID, TOK), F32),
        pltpu.VMEM((HID, 128), F32),
        pltpu.VMEM((HID, 768), F32),
        pltpu.VMEM((16, TOK), F32),
        pltpu.VMEM((16, TOK), F32),
        pltpu.VMEM((8, 8, TOK), F32),
        pltpu.VMEM((16, 2, 96, TOK), BF16),
        pltpu.VMEM((2, 4, 96, TOK), BF16),
        pltpu.VMEM((2, 4, 2, 96, TOK), BF16),
        pltpu.VMEM((4, 2, 96, TOK), BF16),
        pltpu.VMEM((2, 96, TOK), F32),
        pltpu.VMEM((10, 8, TOK), F32),
        pltpu.VMEM((8, 8, 256), F32),
    ]
    scratch += pair(2, 4) + pair(8, 8) + pair(4) + pair(4, 8) + [dma((2,)), dma]
    scratch += pair(2, 2, 4) + pair(2) + pair(2, 2, 4) + pair(2, 2, 4)
    scratch += [pltpu.SemaphoreType.REGULAR] * 4
    scratch += pair(4, 4) + pair(2, 4) + pair(2, 4) + pair(4) + pair(8) + pair(7) + pair(8) + [dma((22,))]
    shapes = (
        jax.ShapeDtypeStruct((ROWS, TOK), BF16),
        jax.ShapeDtypeStruct((1, ROWS), F32),
        jax.ShapeDtypeStruct((768, HID), F32),
        jax.ShapeDtypeStruct((HID, 768), F32),
    )
    results = pl.pallas_call(
        kernel,
        out_shape=shapes,
        in_specs=[anywhere, anywhere, vmem, vmem, anywhere, anywhere],
        out_specs=(vmem, vmem, vmem, anywhere),
        scratch_shapes=scratch,
        compiler_params=pltpu.CompilerParams(
            collective_id=0, has_side_effects=True, vmem_limit_bytes=62 * 2**20
        ),
        cost_estimate=pl.CostEstimate(flops=9 * 10**9, bytes_accessed=12 * 10**6, transcendentals=147456),
        name="parallel_block_backward",
    )(
        block_input.T.reshape(2, 96, TOK),
        output_gradient.T.reshape(2, 96, TOK),
        attn_grad.T.reshape(2, 96, TOK),
        layernorm_gain.reshape(48, 128),
        w_in.reshape(16, CHIP, HID),
        w_out,
    )
    dx, dgain, dw_in, dw_out = pl.pallas_call(
        hand_over,
        out_shape=shapes,
        in_specs=[anywhere] * 4,
        out_specs=(anywhere,) * 4,
        scratch_shapes=[pltpu.VMEM(s.shape, s.dtype) for s in shapes] + [dma((2, 4))],
        name="results",
    )(*results)
    return dx.T, dgain.reshape(ROWS), dw_in, dw_out


def solution(mesh):
    token = P("dp", "tensor")
    return jax.shard_map(
        on_device,
        mesh=mesh,
        in_specs=(token, token, token, P(), P(None, "tensor"), P("tensor", None)),
        out_specs=(token, P("tensor"), P("dp", "tensor"), P("tensor", "dp")),
        check_vma=False,
    )
```
